128 devices in a mesh: dp: 8 (over x, y_lo), ctx: 16 (over y_hi, z, core).
Axes of the slice: x: 4, y: 4 (y_hi: 2, y_lo: 2; y = y_hi * 2 + y_lo), z: 4, core: 2. Of those that a mesh axis runs over, the one named last changes fastest.
Arguments:
- tokens: bfloat16 [32768, 2048], P(('dp', 'ctx'))
- qkv_weight: bfloat16 [2048, 1536], replicated, may hold values from -0.125 to 0.125
- block_place: int32 [8, 32], P('dp'), may hold values from 0 to 31, each once within a row
- seg_ids: int32 [8, 32], P('dp'), may hold values from 0 to 3, never falling along the last dimension, each value on 1 to 16 neighbouring positions
- output_cotangent: bfloat16 [32768, 1024], P(('dp', 'ctx')), may hold values from -6 to 6
Outputs:
- attn_out: bfloat16 [32768, 1024], P(('dp', 'ctx'))
- grad_tokens: bfloat16 [32768, 2048], P(('dp', 'ctx'))
- grad_weight: float32 [2048, 1536], P(('dp', 'ctx'))
The draws below stay inside these ranges and needn't reach their ends.
Inputs may be any that keep to these rules, and one draw needn't show every extreme that they name: `block_place`: each row lists every block number once. `seg_ids`: never falls along a row; each sequence spans 1 to 16 blocks, one exactly 16.
All inputs are finite; a program needn't handle non-finite values.
Results may differ from the reference program's by a relative error of at most 0.01.
The reference program's roundings to bfloat16 on the way count: a program that leaves them out, or rounds other values in their place, can miss the bound.
Values may be sent and summed in bfloat16 or wider, within the bound.
A program may use at most 128 MiB of HBM per device.

```python
import math
import jax
import jax.numpy as jnp
import numpy as np
from jax import lax

D = 2048
QUERY_HEAD_COUNT = 16
KEY_VALUE_HEADS = 4
HEAD_WIDTH = 64
BLK = 128
SEGS = 4
TOK_DEV = 256
WQKV = 1536
NB = 32
MOST_BLK = 16
TOKENS = 32768
N_DP = 8
N_CTX = 16


def draw_tokens(key, part):
    key = jax.random.fold_in(key, 11)
    first = jax.random.fold_in(key, 0)
    base = jax.random.normal(first, (TOKENS, D), jnp.float32)
    return base.astype(jnp.bfloat16)


def shard_levels(stream_key, extent, pieces, least, largest):
    level = 1.0
    for dim, blocks in pieces:
        heights = jax.random.uniform(jax.random.fold_in(jax.random.fold_in(stream_key, 6), dim), (blocks,), jnp.float32, least / len(pieces), largest / len(pieces))
        level = level * jnp.repeat(jnp.exp(heights), extent[dim] // blocks).reshape((-1,) + (1,) * (len(extent) - 1 - dim))
    return level


def profile(number_of, total, most, slope):
    weights = [(1 << 20) // math.isqrt(grade ** slope) + 1 for grade in range(2, number_of + 1)]
    spare, holding = total - most - (number_of - 1), [1] * (number_of - 1)
    while spare > 0:
        candidates = [i for i in range(number_of - 1) if holding[i] < most]
        pool, remaining = sum([weights[i] for i in candidates]), spare
        for i in candidates:
            addition = min(most - holding[i], max(1, remaining * weights[i] // pool), spare)
            holding[i] = holding[i] + addition
            spare = spare - addition
    return np.array([most] + holding)


def uneven(stream_key, amount, total, reach, slope):
    if amount == 2:
        one = jax.random.randint(stream_key, (), max(1, total - reach), min(reach, total - 1) + 1)
        return jnp.stack([one, total - one])
    tallies = jnp.asarray(profile(amount, total, reach, slope), jnp.int32)
    twos = (amount - 1) // 2
    giver, sink = tallies[1:1 + 2 * twos:2], tallies[2:2 + 2 * twos:2]
    margin = jnp.minimum(giver - 1, reach - sink)
    shifted = jax.random.randint(jax.random.fold_in(stream_key, 1), (twos,), 0, 1 << 20) % (margin + 1)
    tallies = tallies.at[1:1 + 2 * twos:2].set(giver - shifted).at[2:2 + 2 * twos:2].set(sink + shifted)
    return tallies[jax.random.permutation(jax.random.fold_in(stream_key, 2), amount)]


def normal_values(own_key, dims, width, most, cuts=(), held_as=jnp.bfloat16):
    result = jax.random.normal(own_key, dims, jnp.float32) * width
    if len(cuts) > 0:
        result = shard_levels(own_key, dims, cuts, -0.22, 0.18) * result
    return jnp.clip(result, min=-most, max=most).astype(held_as)


def setup_inputs(seed: int = 0) -> dict:
    arg_keys = jax.random.split(jax.random.key(seed), 6)
    tokens = draw_tokens(jax.random.fold_in(arg_keys[5], 71), 0)
    qkv_weight = normal_values(arg_keys[1], (D, WQKV), D ** -0.5, 0.125)
    block_place = jax.vmap(lambda own: jax.random.permutation(own, NB))(jax.random.split(arg_keys[2], N_DP)).reshape((N_DP, NB)).astype(jnp.int32)
    seg_ids = jax.vmap(lambda own: jnp.searchsorted(jnp.cumsum(uneven(own, SEGS, NB, MOST_BLK, 2)), jnp.arange(NB), side="right"))(jax.random.split(arg_keys[3], N_DP)).reshape((N_DP, NB)).astype(jnp.int32)
    output_cotangent = normal_values(arg_keys[4], (TOKENS, QUERY_HEAD_COUNT * HEAD_WIDTH), 1.0, 6.0, ((0, 128),))
    return {"tokens": tokens, "qkv_weight": qkv_weight, "block_place": block_place, "seg_ids": seg_ids, "output_cotangent": output_cotangent}


def one_head(allowed, factor, inputs):
    query_head, key_head, value_head, cot_head = inputs
    scores = jnp.dot(query_head, key_head.T, preferred_element_type=jnp.float32) * factor
    scores = jnp.where(allowed, scores, -1e30)
    peak = jnp.max(scores, axis=1, keepdims=True)
    expo = jnp.exp(scores - peak)
    probs = expo / jnp.sum(expo, axis=1, keepdims=True)
    probs_b = probs.astype(jnp.bfloat16)
    output = jnp.dot(probs_b, value_head, preferred_element_type=jnp.float32).astype(jnp.bfloat16)
    grad_probs = jnp.dot(cot_head, value_head.T, preferred_element_type=jnp.float32)
    row_dot = jnp.sum(cot_head.astype(jnp.float32) * output.astype(jnp.float32), axis=1, keepdims=True)
    grad_scores = (probs * (grad_probs - row_dot)).astype(jnp.bfloat16)
    grad_query = jnp.dot(grad_scores, key_head, preferred_element_type=jnp.float32) * factor
    key_gradient = jnp.dot(grad_scores.T, query_head, preferred_element_type=jnp.float32) * factor
    value_gradient = jnp.dot(probs_b.T, cot_head, preferred_element_type=jnp.float32)
    return output, grad_query, key_gradient, value_gradient


def reference(tokens, qkv_weight, block_place, seg_ids, output_cotangent):
    factor = HEAD_WIDTH ** -0.5
    group_count = QUERY_HEAD_COUNT // KEY_VALUE_HEADS
    group_length = TOK_DEV * N_CTX
    query_key_value = jnp.dot(tokens, qkv_weight, preferred_element_type=jnp.float32).astype(jnp.bfloat16)
    query_rows = query_key_value[:, :QUERY_HEAD_COUNT * HEAD_WIDTH].reshape(N_DP, group_length, QUERY_HEAD_COUNT * HEAD_WIDTH)
    key_row_block = query_key_value[:, QUERY_HEAD_COUNT * HEAD_WIDTH:(QUERY_HEAD_COUNT + KEY_VALUE_HEADS) * HEAD_WIDTH].reshape(N_DP, group_length, KEY_VALUE_HEADS * HEAD_WIDTH)
    value_row_block = query_key_value[:, (QUERY_HEAD_COUNT + KEY_VALUE_HEADS) * HEAD_WIDTH:].reshape(N_DP, group_length, KEY_VALUE_HEADS * HEAD_WIDTH)
    cotangent = output_cotangent.reshape(N_DP, group_length, QUERY_HEAD_COUNT * HEAD_WIDTH)

    def one_pack(inputs):
        query_pack, packed_key, packed_value, cot_pack, slot_block, block_seq = inputs
        slot_seq = jnp.take(block_seq, slot_block)
        position = (slot_block[:, None] * BLK + jnp.arange(BLK, dtype=jnp.int32)[None, :]).reshape(group_length)
        seq_tok = jnp.repeat(slot_seq, BLK)
        allowed = (seq_tok[:, None] == seq_tok[None, :]) & (position[None, :] <= position[:, None])
        query_heads = query_pack.reshape(group_length, QUERY_HEAD_COUNT, HEAD_WIDTH).transpose(1, 0, 2)
        key_head_rows = jnp.repeat(packed_key.reshape(group_length, KEY_VALUE_HEADS, HEAD_WIDTH).transpose(1, 0, 2), group_count, axis=0)
        value_head_rows = jnp.repeat(packed_value.reshape(group_length, KEY_VALUE_HEADS, HEAD_WIDTH).transpose(1, 0, 2), group_count, axis=0)
        cot_heads = cot_pack.reshape(group_length, QUERY_HEAD_COUNT, HEAD_WIDTH).transpose(1, 0, 2)
        output, grad_query, key_gradient, value_gradient = lax.map(
            lambda inner: one_head(allowed, factor, inner), (query_heads, key_head_rows, value_head_rows, cot_heads))
        output = output.transpose(1, 0, 2).reshape(group_length, QUERY_HEAD_COUNT * HEAD_WIDTH)
        grad_query = grad_query.transpose(1, 0, 2).reshape(group_length, QUERY_HEAD_COUNT * HEAD_WIDTH)
        key_gradient = key_gradient.reshape(KEY_VALUE_HEADS, group_count, group_length, HEAD_WIDTH).sum(1).transpose(1, 0, 2).reshape(group_length, KEY_VALUE_HEADS * HEAD_WIDTH)
        value_gradient = value_gradient.reshape(KEY_VALUE_HEADS, group_count, group_length, HEAD_WIDTH).sum(1).transpose(1, 0, 2).reshape(group_length, KEY_VALUE_HEADS * HEAD_WIDTH)
        grad_qkv = jnp.concatenate([grad_query, key_gradient, value_gradient], axis=1).astype(jnp.bfloat16)
        return output, grad_qkv

    attn_out, grad_qkv = lax.map(one_pack, (query_rows, key_row_block, value_row_block, cotangent, block_place, seg_ids))
    attn_out = attn_out.reshape(TOKENS, QUERY_HEAD_COUNT * HEAD_WIDTH)
    grad_qkv = grad_qkv.reshape(TOKENS, WQKV)
    grad_tokens = jnp.dot(grad_qkv, qkv_weight.T, preferred_element_type=jnp.float32).astype(jnp.bfloat16)
    grad_weight = jnp.dot(tokens.T, grad_qkv, preferred_element_type=jnp.float32)
    return attn_out, grad_tokens, grad_weight
```

```python
import functools
import jax
import jax.numpy as jnp
from jax import lax
from jax.experimental import pallas as pl
from jax.experimental.pallas import tpu as pltpu
from jax.sharding import PartitionSpec as P

HEADS = 16
KV_HEADS = 4
WIDTH = 64
BLK = 128
ROWS = 256
PACK = 4096
D = 2048
WQKV = 1536
MESH = pl.DeviceIdType.MESH
NT = (((1,), (1,)), ((), ()))
F32 = jnp.float32
BF16 = jnp.bfloat16


def project_kernel(tokens, weight, cot, qo_out, kv_out, tok_out,
                   qo_buf, kv_buf, tok_buf, qo_send, qo_recv, kv_send, kv_recv, tok_send, tok_recv, local):
    dp = lax.axis_index("dp")
    me = lax.axis_index("ctx")
    core = lax.rem(me, 2)
    sibling = me + 1 - 2 * core

    barrier = pltpu.get_barrier_semaphore()
    for step in range(1, HEADS):
        pl.semaphore_signal(barrier, inc=1, device_id=(dp, lax.rem(me + step, HEADS)), device_id_type=MESH)

    def columns(part):
        return jnp.dot(tokens[...], weight[:, part * 256:(part + 1) * 256], preferred_element_type=F32).astype(BF16)

    keys, values = columns(4), columns(5)
    for k in range(KV_HEADS):
        kv_buf[k] = jnp.concatenate([keys[:, k * 64:(k + 1) * 64], values[:, k * 64:(k + 1) * 64]], axis=1)
    pl.semaphore_wait(barrier, HEADS - 1)

    def kv_copy(peer, slot):
        return pltpu.make_async_remote_copy(
            src_ref=kv_buf.at[peer // 4], dst_ref=kv_out.at[slot], send_sem=kv_send.at[peer], recv_sem=kv_recv.at[slot],
            device_id=(dp, peer), device_id_type=MESH)

    def qo_copy(peer, slot):
        return pltpu.make_async_remote_copy(
            src_ref=qo_buf.at[peer], dst_ref=qo_out.at[slot], send_sem=qo_send.at[peer], recv_sem=qo_recv.at[slot],
            device_id=(dp, peer), device_id_type=MESH)

    kv_local = pltpu.make_async_copy(kv_buf.at[me // 4], kv_out.at[me], local.at[0])
    qo_local = pltpu.make_async_copy(qo_buf.at[me], qo_out.at[me], local.at[1])
    tok_local = pltpu.make_async_copy(tok_buf.at[core], tok_out.at[core], local.at[2])
    kv_local.start()
    for step in range(1, HEADS):
        kv_copy(lax.rem(me + step, HEADS), me).start()
    for part in range(4):
        queries = columns(part)
        for i in range(4):
            h = part * 4 + i
            qo_buf[h] = jnp.concatenate(
                [queries[:, i * 64:(i + 1) * 64] * 0.125, cot[:, h * 64:(h + 1) * 64]], axis=1)
    qo_local.start()
    for step in range(1, HEADS):
        qo_copy(lax.rem(me + step, HEADS), me).start()
    for part in range(8):
        turned = tokens[:, part * 256:(part + 1) * 256].T
        for g in range(8):
            for c in range(2):
                tok_buf[c, part * 128 + g * 16: part * 128 + (g + 1) * 16, :] = turned[(2 * g + c) * 16:(2 * g + c + 1) * 16, :]
    tok_local.start()
    tok_copy = pltpu.make_async_remote_copy(
        src_ref=tok_buf.at[1 - core], dst_ref=tok_out.at[core], send_sem=tok_send, recv_sem=tok_recv,
        device_id=(dp, sibling), device_id_type=MESH)
    tok_copy.start()
    for step in range(1, HEADS):
        peer = lax.rem(me + step, HEADS)
        kv_copy(peer, me).wait_send()
        qo_copy(peer, me).wait_send()
        kv_copy(peer, peer).wait_recv()
        qo_copy(peer, peer).wait_recv()
    tok_copy.wait_send()
    pltpu.make_async_remote_copy(
        src_ref=tok_buf.at[1 - core], dst_ref=tok_out.at[1 - core], send_sem=tok_send, recv_sem=tok_recv,
        device_id=(dp, sibling), device_id_type=MESH).wait_recv()
    kv_local.wait()
    qo_local.wait()
    tok_local.wait()


def project(tokens, weight, cot):
    vmem = pl.BlockSpec(memory_space=pltpu.VMEM)
    hbm = pl.BlockSpec(memory_space=pl.ANY)
    return pl.pallas_call(
        project_kernel,
        out_shape=[
            jax.ShapeDtypeStruct((HEADS, ROWS, 128), BF16),
            jax.ShapeDtypeStruct((HEADS, ROWS, 128), BF16),
            jax.ShapeDtypeStruct((2, D // 2, ROWS), BF16),
        ],
        in_specs=[vmem] * 3,
        out_specs=[hbm] * 3,
        scratch_shapes=[
            pltpu.VMEM((HEADS, ROWS, 128), BF16),
            pltpu.VMEM((KV_HEADS, ROWS, 128), BF16),
            pltpu.VMEM((2, D // 2, ROWS), BF16),
            pltpu.SemaphoreType.DMA((HEADS,)),
            pltpu.SemaphoreType.DMA((HEADS,)),
            pltpu.SemaphoreType.DMA((HEADS,)),
            pltpu.SemaphoreType.DMA((HEADS,)),
            pltpu.SemaphoreType.DMA,
            pltpu.SemaphoreType.DMA,
            pltpu.SemaphoreType.DMA((3,)),
        ],
        compiler_params=pltpu.CompilerParams(collective_id=0, has_side_effects=True, vmem_limit_bytes=48 << 20),
        cost_estimate=pl.CostEstimate(flops=2 * ROWS * D * WQKV, bytes_accessed=16 << 20, transcendentals=0),
        name="project",
    )(tokens, weight, cot)


TILE = 256
MOST = 9
NEG = -1e30


def attend_kernel(place, seg, qo, kv, oq, gkv, where_, first, x_buf, qo_t, kv_log, kv_t, grad, score, dprob, expo, pair):
    def invert(slot, _):
        where_[place[0, slot]] = slot
        return 0
    lax.fori_loop(0, 32, invert, 0)
    first[0] = 0

    def starts(b, _):
        first[b] = jnp.where(seg[0, b] == seg[0, b - 1], first[b - 1], b)
        return 0
    lax.fori_loop(1, 32, starts, 0)

    def reorder(b, _):
        slot = where_[b]
        src = pl.ds(pl.multiple_of(slot * BLK, BLK), BLK)
        dst = pl.ds(pl.multiple_of(b * BLK, BLK), BLK)
        both = qo[src, :]
        lane = lax.broadcasted_iota(jnp.int32, (BLK, 128), 1)
        zero = jnp.zeros_like(both)
        tile, half = b // 2, lax.rem(b, 2)
        row = tile * 512 + half * BLK
        x_buf[pl.ds(pl.multiple_of(row, BLK), BLK), :] = jnp.where(lane < 64, both, zero)
        x_buf[pl.ds(pl.multiple_of(row + 256, BLK), BLK), :] = jnp.where(lane < 64, zero, both)
        qo_t[:, dst] = both.T
        block = kv[src, :]
        kv_log[dst, :] = block
        kv_t[:, dst] = block.T
        grad[dst, :] = jnp.zeros((BLK, 128), F32)
        return 0
    lax.fori_loop(0, 32, reorder, 0)

    key_row = lax.broadcasted_iota(jnp.int32, (TILE, TILE), 0)
    lane_row = lax.broadcasted_iota(jnp.int32, (1, TILE), 1)

    def one_tile(t, _):
        first0, first1 = first[2 * t], first[2 * t + 1]
        begin = first0 // 2
        x = x_buf[pl.ds(pl.multiple_of(t * 512, 512), 512), :]
        q_at = lane_row + t * TILE
        q_start = jnp.where(lane_row < BLK, first0 * BLK, first1 * BLK)

        def scores(c, peak):
            both = lax.dot_general(
                kv_log[pl.ds(pl.multiple_of(c * TILE, TILE), TILE), :], x, NT, preferred_element_type=F32)
            k_at = key_row + c * TILE
            s = jnp.where((k_at <= q_at) & (k_at >= q_start), both[:, :TILE], NEG)
            score[c - begin] = s
            dprob[c - begin] = both[:, TILE:]
            return jnp.maximum(peak, jnp.max(s.reshape(TILE // 8, 8, TILE), axis=0))
        peak = lax.fori_loop(begin, t + 1, scores, jnp.full((8, TILE), NEG, F32))
        peak = jnp.max(peak, axis=0, keepdims=True)

        def exps(c, total):
            e = jnp.exp(score[c - begin] - peak)
            score[c - begin] = e
            return total + jnp.sum(e.reshape(TILE // 8, 8, TILE), axis=0)
        total = lax.fori_loop(begin, t + 1, exps, jnp.zeros((8, TILE), F32))
        inv = 1.0 / jnp.sum(total, axis=0, keepdims=True)

        def outs(c, acc):
            p = score[c - begin] * inv
            score[c - begin] = p
            pb = p.astype(BF16)
            pair[c - begin, :, TILE:] = pb
            return acc + jnp.dot(kv_t[64:, pl.ds(pl.multiple_of(c * TILE, TILE), TILE)], pb, preferred_element_type=F32)
        out_t = lax.fori_loop(begin, t + 1, outs, jnp.zeros((64, TILE), F32)).astype(BF16)
        cot_t = qo_t[64:, pl.ds(pl.multiple_of(t * TILE, TILE), TILE)]
        dots = jnp.sum(cot_t.astype(F32) * out_t.astype(F32), axis=0, keepdims=True)

        def grads(c, acc):
            g = (score[c - begin] * (dprob[c - begin] - dots)).astype(BF16)
            pair[c - begin, :, :TILE] = g
            rows = pl.ds(pl.multiple_of(c * TILE, TILE), TILE)
            grad[rows, :] += jnp.dot(pair[c - begin], x, preferred_element_type=F32)
            return acc + jnp.dot(kv_t[:64, rows], g, preferred_element_type=F32)
        dq_t = (lax.fori_loop(begin, t + 1, grads, jnp.zeros((64, TILE), F32)) * 0.125).astype(BF16)
        both = jnp.concatenate([out_t, dq_t], axis=0).T
        for half in range(2):
            slot = where_[2 * t + half]
            oq[pl.ds(pl.multiple_of(slot * BLK, BLK), BLK), :] = both[half * BLK:(half + 1) * BLK]
        return 0
    lax.fori_loop(0, PACK // TILE, one_tile, 0)

    def finish(slot, _):
        gkv[pl.ds(pl.multiple_of(slot * BLK, BLK), BLK), :] = grad[pl.ds(pl.multiple_of(place[0, slot] * BLK, BLK), BLK), :]
        return 0
    lax.fori_loop(0, 32, finish, 0)


def attend(place, seg, qo, kv):
    vmem = pl.BlockSpec(memory_space=pltpu.VMEM)
    smem = pl.BlockSpec(memory_space=pltpu.SMEM)
    return pl.pallas_call(
        attend_kernel,
        out_shape=[jax.ShapeDtypeStruct((PACK, 128), BF16), jax.ShapeDtypeStruct((PACK, 128), F32)],
        in_specs=[smem, smem, vmem, vmem],
        out_specs=[vmem, vmem],
        scratch_shapes=[
            pltpu.SMEM((32,), jnp.int32),
            pltpu.SMEM((32,), jnp.int32),
            pltpu.VMEM((2 * PACK, 128), BF16),
            pltpu.VMEM((128, PACK), BF16),
            pltpu.VMEM((PACK, 128), BF16),
            pltpu.VMEM((128, PACK), BF16),
            pltpu.VMEM((PACK, 128), F32),
            pltpu.VMEM((MOST, TILE, TILE), F32),
            pltpu.VMEM((MOST, TILE, TILE), F32),
            pltpu.VMEM((8, 128), F32),
            pltpu.VMEM((MOST, TILE, 2 * TILE), BF16),
        ],
        compiler_params=pltpu.CompilerParams(vmem_limit_bytes=48 << 20),
        cost_estimate=pl.CostEstimate(flops=10 << 30, bytes_accessed=5 << 20, transcendentals=4 << 20),
        name="attend",
    )(place, seg, qo, kv)


AXES = (("z", "y", "x"), ("y", "x", "z"), ("x", "z", "y"))
THIRD = WQKV // 3


def spread_kernel(oq, gkv, tok, weight, attn, grad_tokens, grad_weight,
                  weight_buf, oq_in, pair_in, pair_sum, kv_in, tok_perm, gq, first_out, first_in, second_out, second_in,
                  third_out, third_in, weight_sem, pair_sems, oq_send, oq_recv, kv_send, kv_recv, gq_sems,
                  first_send, first_recv, second_send, second_recv, third_send, third_recv, local):
    dp = lax.axis_index("dp")
    me = lax.axis_index("ctx")
    core = lax.rem(me, 2)
    chip = me // 2
    sibling = (dp, me + 1 - 2 * core)
    place = {"x": dp // 2, "y": (me // 8) * 2 + lax.rem(dp, 2), "z": lax.rem(chip, 4)}

    def neighbour(axis, offset):
        at = lax.rem(place[axis] + offset, 4)
        if axis == "x":
            return (at * 2 + lax.rem(dp, 2), me)
        if axis == "y":
            return ((dp // 2) * 2 + lax.rem(at, 2), (at // 2) * 8 + lax.rem(me, 8))
        return (dp, (me // 8) * 8 + at * 2 + core)

    barrier = pltpu.get_barrier_semaphore()
    greet = [(dp, lax.rem(me + step, HEADS)) for step in range(1, HEADS)]
    greet += [neighbour("x", step) for step in (1, 2, 3)] + [neighbour("y", step) for step in (1, 3)]
    for device in greet:
        pl.semaphore_signal(barrier, inc=1, device_id=device, device_id_type=MESH)
    weight_copy = pltpu.make_async_copy(weight, weight_buf, weight_sem)
    weight_copy.start()
    pl.semaphore_wait(barrier, len(greet))

    def remote(src, dst, send, recv, device):
        return pltpu.make_async_remote_copy(
            src_ref=src, dst_ref=dst, send_sem=send, recv_sem=recv, device_id=device, device_id_type=MESH)

    pair_copy = remote(gkv.at[:, 1 - core], pair_in, pair_sems.at[0], pair_sems.at[1], sibling)
    pair_copy.start()
    oq_local = pltpu.make_async_copy(oq.at[me], oq_in.at[me], local)
    oq_local.start()

    def oq_copy(peer, slot):
        return remote(oq.at[peer], oq_in.at[slot], oq_send.at[peer], oq_recv.at[slot], (dp, peer))

    def kv_copy(to, slot):
        return remote(pair_sum.at[to], kv_in.at[slot], kv_send.at[to], kv_recv.at[slot], (dp, to * 2 + core))

    for step in range(1, HEADS):
        oq_copy(lax.rem(me + step, HEADS), me).start()
    pair_copy.wait()
    for step in range(1, 9):
        to = lax.rem(chip + step, 8)
        total = gkv[to, core] + pair_in[to]
        if step < 8:
            pair_sum[to] = total
            kv_copy(to, chip).start()
        else:
            kv_in[chip] = total

    for part, order in enumerate(AXES):
        for a in range(4):
            for b in range(4):
                for c in range(4):
                    at = dict(zip(order, (a, b, c)))
                    group = at["x"] * 16 + (at["y"] % 2) * 8 + (at["y"] // 2) * 4 + at["z"]
                    for half in range(2):
                        tok_perm[part, a, (b * 4 + c) * 16:(b * 4 + c + 1) * 16, half * ROWS:(half + 1) * ROWS] = (
                            tok[half, group * 16:(group + 1) * 16, :])

    for step in range(1, HEADS):
        peer = lax.rem(me + step, HEADS)
        oq_copy(peer, peer).wait_recv()
    oq_local.wait()
    for step in range(1, 8):
        src = lax.rem(chip + step, 8)
        kv_copy(src, src).wait_recv()

    mine = gq.at[core]
    for i in range(HEADS // 2):
        mine[:, i * 128:(i + 1) * 128] = jnp.concatenate([oq_in[2 * i, :, 64:], oq_in[2 * i + 1, :, 64:]], axis=1)
    for i in range(KV_HEADS // 2):
        sums = [(kv_in[4 * i + 2 * j] + kv_in[4 * i + 2 * j + 1]).astype(BF16) for j in range(2)]
        mine[:, 1024 + i * 128:1024 + (i + 1) * 128] = jnp.concatenate([s[:, :64] for s in sums], axis=1)
        mine[:, 1280 + i * 128:1280 + (i + 1) * 128] = jnp.concatenate([s[:, 64:] for s in sums], axis=1)
    gq_copy = remote(mine, mine, gq_sems.at[0], gq_sems.at[1], sibling)
    gq_copy.start()
    for i in range(HEADS // 2):
        attn[:, i * 128:(i + 1) * 128] = jnp.concatenate([oq_in[2 * i, :, :64], oq_in[2 * i + 1, :, :64]], axis=1)
    gq_copy.wait_send()
    remote(gq.at[1 - core], gq.at[1 - core], gq_sems.at[0], gq_sems.at[1], sibling).wait_recv()

    def stage_copy(out, came, send, recv, part, level, offset):
        axis = AXES[part][level]
        to = lax.rem(place[axis] + offset, 4)
        return remote(out.at[part, to], came.at[part, offset - 1], send.at[part, offset - 1], recv.at[part, offset - 1],
                      neighbour(axis, offset))

    def first(part, offset):
        return stage_copy(first_out, first_in, first_send, first_recv, part, 0, offset)

    def second(part, offset):
        return stage_copy(second_out, second_in, second_send, second_recv, part, 1, offset)

    def third(part, offset):
        return stage_copy(third_out, third_in, third_send, third_recv, part, 2, offset)

    for offset in (2, 1, 3, 0):
        for part in range(3):
            to = lax.rem(place[AXES[part][0]] + offset, 4)
            cols = slice(part * THIRD, (part + 1) * THIRD)
            rows = tok_perm.at[part, to]
            first_out[part, to] = (
                jnp.dot(rows[:, :ROWS], gq[0, :, cols], preferred_element_type=F32)
                + jnp.dot(rows[:, ROWS:], gq[1, :, cols], preferred_element_type=F32))
            if offset:
                first(part, offset).start()

    weight_copy.wait()
    for part in range(8):
        grad_tokens[:, part * 256:(part + 1) * 256] = lax.dot_general(
            mine[...], weight_buf[part * 256:(part + 1) * 256, :], NT, preferred_element_type=F32).astype(BF16)

    for part in range(3):
        own = lax.rem(place[AXES[part][0]], 4)
        for offset in (1, 2, 3):
            first(part, offset).wait_recv()
        for b in range(4):
            rows = slice(b * 64, (b + 1) * 64)
            second_out[part, b] = (first_out[part, own, rows] + first_in[part, 0, rows]
                                   + first_in[part, 1, rows] + first_in[part, 2, rows])
        for offset in (2, 1, 3):
            second(part, offset).start()
    for part in range(3):
        own = lax.rem(place[AXES[part][1]], 4)
        for offset in (1, 2, 3):
            second(part, offset).wait_recv()
        for c in range(4):
            rows = slice(c * 16, (c + 1) * 16)
            third_out[part, c] = (second_out[part, own, rows] + second_in[part, 0, rows]
                                  + second_in[part, 1, rows] + second_in[part, 2, rows])
        for offset in (2, 1, 3):
            third(part, offset).start()
    for part in range(3):
        own = lax.rem(place[AXES[part][2]], 4)
        for offset in (1, 2, 3):
            third(part, offset).wait_recv()
        grad_weight[:, part * THIRD:(part + 1) * THIRD] = (
            third_out[part, own] + third_in[part, 0] + third_in[part, 1] + third_in[part, 2])

    for step in range(1, HEADS):
        oq_copy(lax.rem(me + step, HEADS), me).wait_send()
    for step in range(1, 8):
        kv_copy(lax.rem(chip + step, 8), chip).wait_send()
    for part in range(3):
        for offset in (1, 2, 3):
            first(part, offset).wait_send()
            second(part, offset).wait_send()
            third(part, offset).wait_send()


def spread(oq, gkv, tok, weight):
    vmem = pl.BlockSpec(memory_space=pltpu.VMEM)
    hbm = pl.BlockSpec(memory_space=pl.ANY)
    sem = pltpu.SemaphoreType.DMA
    return pl.pallas_call(
        spread_kernel,
        out_shape=[
            jax.ShapeDtypeStruct((ROWS, 1024), BF16),
            jax.ShapeDtypeStruct((ROWS, D), BF16),
            jax.ShapeDtypeStruct((16, WQKV), F32),
        ],
        in_specs=[hbm, vmem, vmem, hbm],
        out_specs=[vmem] * 3,
        scratch_shapes=[
            pltpu.VMEM((D, WQKV), BF16),
            pltpu.VMEM((HEADS, ROWS, 128), BF16),
            pltpu.VMEM((8, ROWS, 128), F32),
            pltpu.VMEM((8, ROWS, 128), F32),
            pltpu.VMEM((8, ROWS, 128), F32),
            pltpu.VMEM((3, 4, 256, 2 * ROWS), BF16),
            pltpu.VMEM((2, ROWS, WQKV), BF16),
            pltpu.VMEM((3, 4, 256, THIRD), F32),
            pltpu.VMEM((3, 3, 256, THIRD), F32),
            pltpu.VMEM((3, 4, 64, THIRD), F32),
            pltpu.VMEM((3, 3, 64, THIRD), F32),
            pltpu.VMEM((3, 4, 16, THIRD), F32),
            pltpu.VMEM((3, 3, 16, THIRD), F32),
            sem, sem((2,)), sem((HEADS,)), sem((HEADS,)), sem((8,)), sem((8,)), sem((2,)),
            sem((3, 3)), sem((3, 3)), sem((3, 3)), sem((3, 3)), sem((3, 3)), sem((3, 3)), sem,
        ],
        compiler_params=pltpu.CompilerParams(collective_id=1, has_side_effects=True, vmem_limit_bytes=56 << 20),
        cost_estimate=pl.CostEstimate(flops=4 * ROWS * D * WQKV, bytes_accessed=16 << 20, transcendentals=0),
        name="spread",
    )(oq, gkv, tok, weight)


def shards(tokens, qkv_weight, block_place, seg_ids, output_cotangent):
    qo, kv, tok = project(tokens, qkv_weight, output_cotangent)
    oq, gkv = attend(block_place, seg_ids, qo.reshape(PACK, 128), kv.reshape(PACK, 128))
    return tuple(spread(oq.reshape(HEADS, ROWS, 128), gkv.reshape(8, 2, ROWS, 128), tok, qkv_weight))


def solution(mesh):
    placed = (P(("dp", "ctx"), None), P(), P("dp", None), P("dp", None), P(("dp", "ctx"), None))
    return jax.shard_map(
        shards,
        mesh=mesh,
        in_specs=placed,
        out_specs=(P(("dp", "ctx"), None), P(("dp", "ctx"), None), P(("dp", "ctx"), None)),
        check_vma=False,
    )
```

```python
import functools
import jax
import jax.numpy as jnp
from jax import lax
from jax.experimental import pallas as pl
from jax.experimental.pallas import tpu as pltpu
from jax.sharding import PartitionSpec as P

HEADS = 16
KV_HEADS = 4
WIDTH = 64
BLK = 128
ROWS = 256
PACK = 4096
D = 2048
WQKV = 1536
MESH = pl.DeviceIdType.MESH
NT = (((1,), (1,)), ((), ()))
F32 = jnp.float32
BF16 = jnp.bfloat16


def project_kernel(tokens_in, weight_in, cot_in, q_out, cot_out, kv_out, tok_out,
                   tokens, weight, cot, q_buf, cot_buf, kv_buf, tok_buf,
                   q_send, q_recv, cot_send, cot_recv, kv_send, kv_recv, tok_send, tok_recv, fetched, local):
    dp = lax.axis_index("dp")
    me = lax.axis_index("ctx")
    core = lax.rem(me, 2)
    sibling = me + 1 - 2 * core

    barrier = pltpu.get_barrier_semaphore()
    for step in range(1, HEADS):
        pl.semaphore_signal(barrier, inc=1, device_id=(dp, lax.rem(me + step, HEADS)), device_id_type=MESH)
    fetches = [
        pltpu.make_async_copy(cot_in, cot, fetched.at[0]),
        pltpu.make_async_copy(tokens_in, tokens, fetched.at[1]),
        pltpu.make_async_copy(weight_in.at[:, 1024:], weight.at[:, 1024:], fetched.at[2]),
        pltpu.make_async_copy(weight_in.at[:, :1024], weight.at[:, :1024], fetched.at[3]),
    ]
    for fetch in fetches:
        fetch.start()

    def remote(src, dst, send, recv, peer):
        return pltpu.make_async_remote_copy(
            src_ref=src, dst_ref=dst, send_sem=send, recv_sem=recv, device_id=(dp, peer), device_id_type=MESH)

    def cot_copy(peer, slot):
        return remote(cot_buf.at[peer], cot_out.at[slot], cot_send.at[peer], cot_recv.at[slot], peer)

    def q_copy(peer, slot):
        return remote(q_buf.at[peer], q_out.at[slot], q_send.at[peer], q_recv.at[slot], peer)

    def kv_copy(peer, slot):
        return remote(kv_buf.at[peer // 4], kv_out.at[slot], kv_send.at[peer], kv_recv.at[slot], peer)

    def kv_forward(slot):
        return remote(kv_out.at[slot], kv_out.at[slot], kv_send.at[slot + 1 - 2 * core], kv_recv.at[slot], sibling)

    def fold_rows(columns):
        return jnp.concatenate([columns[:BLK], columns[BLK:]], axis=1)

    fetches[0].wait()
    for h in range(HEADS):
        cot_buf[h] = fold_rows(cot[:, h * 64:(h + 1) * 64])
    pl.semaphore_wait(barrier, HEADS - 1)
    locals_ = [
        pltpu.make_async_copy(cot_buf.at[me], cot_out.at[me], local.at[0]),
        pltpu.make_async_copy(kv_buf.at[me // 4], kv_out.at[me], local.at[1]),
        pltpu.make_async_copy(q_buf.at[me], q_out.at[me], local.at[2]),
        pltpu.make_async_copy(tok_buf.at[core], tok_out.at[core], local.at[3]),
    ]
    locals_[0].start()
    for step in range(1, HEADS):
        cot_copy(lax.rem(me + step, HEADS), me).start()

    def columns(part):
        return jnp.dot(tokens[...], weight[:, part * 256:(part + 1) * 256], preferred_element_type=F32).astype(BF16)

    fetches[1].wait()
    fetches[2].wait()
    keys, values = columns(4), columns(5)
    for k in range(KV_HEADS):
        kv_buf[k] = jnp.concatenate([keys[:, k * 64:(k + 1) * 64], values[:, k * 64:(k + 1) * 64]], axis=1)
    locals_[1].start()
    for step in range(1, 8):
        kv_copy(lax.rem(me + 2 * step, HEADS), me).start()
    kv_copy(sibling, me).start()
    fetches[3].wait()
    for part in range(4):
        queries = columns(part)
        for i in range(4):
            q_buf[part * 4 + i] = fold_rows(queries[:, i * 64:(i + 1) * 64] * 0.125)
    locals_[2].start()
    for step in range(1, HEADS):
        q_copy(lax.rem(me + step, HEADS), me).start()
    for part in range(8):
        turned = tokens[:, part * 256:(part + 1) * 256].T
        for g in range(8):
            for c in range(2):
                tok_buf[c, part * 128 + g * 16: part * 128 + (g + 1) * 16, :] = turned[(2 * g + c) * 16:(2 * g + c + 1) * 16, :]
    locals_[3].start()
    tok_copy = remote(tok_buf.at[1 - core], tok_out.at[core], tok_send, tok_recv, sibling)
    tok_copy.start()
    for step in range(1, 8):
        src = lax.rem(me + HEADS - 2 * step, HEADS)
        kv_copy(src, src).wait_recv()
        kv_forward(src).start()
    for step in range(1, HEADS):
        src = lax.rem(me + HEADS - step, HEADS)
        cot_copy(src, src).wait_recv()
        q_copy(src, src).wait_recv()
    kv_copy(sibling, sibling).wait_recv()
    for step in range(1, 8):
        src = lax.rem(sibling + HEADS - 2 * step, HEADS)
        kv_copy(src, src).wait_recv()
    remote(tok_buf.at[1 - core], tok_out.at[1 - core], tok_send, tok_recv, sibling).wait_recv()
    tok_copy.wait_send()
    for step in range(1, HEADS):
        peer = lax.rem(me + step, HEADS)
        cot_copy(peer, me).wait_send()
        q_copy(peer, me).wait_send()
    for step in range(1, 8):
        peer = lax.rem(me + 2 * step, HEADS)
        kv_copy(peer, me).wait_send()
        kv_forward(peer).wait_send()
    kv_copy(sibling, me).wait_send()
    for copy in locals_:
        copy.wait()


def project(tokens, weight, cot):
    hbm = pl.BlockSpec(memory_space=pltpu.HBM)
    sem = pltpu.SemaphoreType.DMA
    return pl.pallas_call(
        project_kernel,
        out_shape=[
            jax.ShapeDtypeStruct((HEADS, BLK, 128), BF16),
            jax.ShapeDtypeStruct((HEADS, BLK, 128), BF16),
            jax.ShapeDtypeStruct((HEADS, ROWS, 128), BF16),
            jax.ShapeDtypeStruct((2, D // 2, ROWS), BF16),
        ],
        in_specs=[hbm] * 3,
        out_specs=[hbm] * 4,
        scratch_shapes=[
            pltpu.VMEM((ROWS, D), BF16),
            pltpu.VMEM((D, WQKV), BF16),
            pltpu.VMEM((ROWS, 1024), BF16),
            pltpu.VMEM((HEADS, BLK, 128), BF16),
            pltpu.VMEM((HEADS, BLK, 128), BF16),
            pltpu.VMEM((KV_HEADS, ROWS, 128), BF16),
            pltpu.VMEM((2, D // 2, ROWS), BF16),
            sem((HEADS,)), sem((HEADS,)), sem((HEADS,)), sem((HEADS,)), sem((HEADS,)), sem((HEADS,)),
            sem, sem, sem((4,)), sem((4,)),
        ],
        compiler_params=pltpu.CompilerParams(collective_id=0, has_side_effects=True, vmem_limit_bytes=48 << 20),
        cost_estimate=pl.CostEstimate(flops=2 * ROWS * D * WQKV, bytes_accessed=16 << 20, transcendentals=0),
        name="project",
    )(tokens, weight, cot)


TILE = 256
MOST = 9
SIZES = (4, 2, 1)
NEG = -1e30


def attend_kernel(place, seg, q_in, cot_in, kv_in, out, dq, gkv,
                  q, cot, kv, where_, first, x_buf, cot_t, kv_log, kv_t, grad, score, pair, fetched):
    fetches = [pltpu.make_async_copy(src, dst, fetched.at[i])
               for i, (src, dst) in enumerate(((kv_in, kv), (q_in, q), (cot_in, cot)))]
    for fetch in fetches:
        fetch.start()

    def invert(slot, _):
        where_[place[0, slot]] = slot
        return 0
    lax.fori_loop(0, 32, invert, 0)
    first[0] = 0

    def starts(b, _):
        first[b] = jnp.where(seg[0, b] == seg[0, b - 1], first[b - 1], b)
        return 0
    lax.fori_loop(1, 32, starts, 0)

    lane = lax.broadcasted_iota(jnp.int32, (BLK, 128), 1)
    for fetch in fetches:
        fetch.wait()

    def reorder(tile, _):
        for part in range(2):
            b = 2 * tile + part
            slot = where_[b]
            half = lax.rem(slot, 2)
            dst = pl.ds(pl.multiple_of(b * BLK, BLK), BLK)
            row = tile * 512 + part * BLK
            mine = q[slot // 2]
            mine = jnp.where(half == 0, mine, jnp.concatenate([mine[:, 64:], mine[:, :64]], axis=1))
            x_buf[pl.ds(pl.multiple_of(row, BLK), BLK), :] = jnp.where(lane < 64, mine, jnp.zeros_like(mine))
            mine = cot[slot // 2]
            mine = jnp.where(half == 1, mine, jnp.concatenate([mine[:, 64:], mine[:, :64]], axis=1))
            x_buf[pl.ds(pl.multiple_of(row + 256, BLK), BLK), :] = jnp.where(lane < 64, jnp.zeros_like(mine), mine)
            cot_t[:, dst] = mine.T[64:]
            block = kv[pl.ds(pl.multiple_of(slot * BLK, BLK), BLK), :]
            kv_log[dst, :] = block
            kv_t[:, dst] = block.T
            grad[dst, :] = jnp.zeros((BLK, 128), F32)
        return 0
    lax.fori_loop(0, 16, reorder, 0)

    key_row = lax.broadcasted_iota(jnp.int32, (TILE, TILE), 0)
    lane_row = lax.broadcasted_iota(jnp.int32, (1, TILE), 1)

    def rows_of(c, size=1):
        return pl.ds(pl.multiple_of(c * TILE, TILE), size * TILE)

    def fold(s, op):
        return op(s.reshape(s.shape[0] // 8, 8, TILE), axis=0)

    def sweep(count, body, carry):
        at = 0
        for size in SIZES:
            steps = (count - at) // size
            carry = lax.fori_loop(0, steps, lambda i, carry, at=at, size=size: body(at + i * size, size, carry), carry)
            at = at + steps * size
        return carry

    def one_tile(t, _):
        first0, first1 = first[2 * t], first[2 * t + 1]
        begin = first0 // 2
        count = t - begin + 1
        x = x_buf.at[pl.ds(pl.multiple_of(t * 512, 512), 512), :]
        q_first = jnp.where(lane_row < BLK, first0, first1)

        def scores(i, size, carry):
            peak, total = carry
            c = begin + i
            s = lax.dot_general(kv_log[rows_of(c, size), :], x[:TILE, :], NT, preferred_element_type=F32)
            s = jnp.concatenate([
                s[b * BLK:(b + 1) * BLK] + jnp.where(q_first <= 2 * c + b, 0.0, NEG) for b in range(2 * size)], axis=0)
            score[rows_of(i, size), :] = s
            new = jnp.maximum(peak, jnp.max(fold(s, jnp.max), axis=0, keepdims=True))
            total = total * jnp.exp(peak - new) + fold(jnp.exp(s - new), jnp.sum)
            return new, total

        s = lax.dot_general(kv_log[rows_of(t), :], x[:TILE, :], NT, preferred_element_type=F32)
        s = jnp.where((key_row <= lane_row) & (key_row >= (q_first - 2 * t) * BLK), s, NEG)
        score[rows_of(count - 1), :] = s
        peak = jnp.max(fold(s, jnp.max), axis=0, keepdims=True)
        total = fold(jnp.exp(s - peak), jnp.sum)
        peak, total = sweep(count - 1, scores, (peak, total))
        inv = 1.0 / jnp.sum(total, axis=0, keepdims=True)

        def outs(i, size, acc):
            p = jnp.exp(score[rows_of(i, size), :] - peak) * inv
            score[rows_of(i, size), :] = p
            pb = p.astype(BF16)
            pair[rows_of(i, size), TILE:] = pb
            return acc + jnp.dot(kv_t[64:, rows_of(begin + i, size)], pb, preferred_element_type=F32)
        out_t = sweep(count, outs, jnp.zeros((64, TILE), F32)).astype(BF16)
        dots = jnp.sum(cot_t[:, rows_of(t)].astype(F32) * out_t.astype(F32), axis=0, keepdims=True)

        def grads(i, size, acc):
            rows = rows_of(begin + i, size)
            dp = lax.dot_general(kv_log[rows, :], x[TILE:, :], NT, preferred_element_type=F32)
            g = (score[rows_of(i, size), :] * (dp - dots)).astype(BF16)
            pair[rows_of(i, size), :TILE] = g
            grad[rows, :] += jnp.dot(pair[rows_of(i, size), :], x[...], preferred_element_type=F32)
            return acc + jnp.dot(kv_t[:64, rows], g, preferred_element_type=F32)
        dq_t = (sweep(count, grads, jnp.zeros((64, TILE), F32)) * 0.125).astype(BF16)
        for part in range(2):
            slot = where_[2 * t + part]
            side = (lane < 64) == (lax.rem(slot, 2) == 0)
            for turned, to in ((out_t, out), (dq_t, dq)):
                block = turned[:, part * BLK:(part + 1) * BLK]
                block = jnp.concatenate([block, block], axis=0).T
                to[slot // 2] = jnp.where(side, block, to[slot // 2])
        return 0
    lax.fori_loop(0, PACK // TILE, one_tile, 0)

    def finish(slot, _):
        gkv[pl.ds(pl.multiple_of(slot * BLK, BLK), BLK), :] = grad[pl.ds(pl.multiple_of(place[0, slot] * BLK, BLK), BLK), :]
        return 0
    lax.fori_loop(0, 32, finish, 0)


def attend(place, seg, q, cot, kv):
    vmem = pl.BlockSpec(memory_space=pltpu.VMEM)
    smem = pl.BlockSpec(memory_space=pltpu.SMEM)
    hbm = pl.BlockSpec(memory_space=pltpu.HBM)
    return pl.pallas_call(
        attend_kernel,
        out_shape=[
            jax.ShapeDtypeStruct((HEADS, BLK, 128), BF16),
            jax.ShapeDtypeStruct((HEADS, BLK, 128), BF16),
            jax.ShapeDtypeStruct((PACK, 128), F32),
        ],
        in_specs=[smem, smem, hbm, hbm, hbm],
        out_specs=[vmem] * 3,
        scratch_shapes=[
            pltpu.VMEM((HEADS, BLK, 128), BF16),
            pltpu.VMEM((HEADS, BLK, 128), BF16),
            pltpu.VMEM((PACK, 128), BF16),
            pltpu.SMEM((32,), jnp.int32),
            pltpu.SMEM((32,), jnp.int32),
            pltpu.VMEM((2 * PACK, 128), BF16),
            pltpu.VMEM((64, PACK), BF16),
            pltpu.VMEM((PACK, 128), BF16),
            pltpu.VMEM((128, PACK), BF16),
            pltpu.VMEM((PACK, 128), F32),
            pltpu.VMEM((MOST * TILE, TILE), F32),
            pltpu.VMEM((MOST * TILE, 2 * TILE), BF16),
            pltpu.SemaphoreType.DMA((3,)),
        ],
        compiler_params=pltpu.CompilerParams(vmem_limit_bytes=48 << 20),
        cost_estimate=pl.CostEstimate(flops=10 << 30, bytes_accessed=5 << 20, transcendentals=4 << 20),
        name="attend",
    )(place, seg, q, cot, kv)


AXES = (("z", "y", "x"), ("y", "x", "z"), ("x", "z", "y"))
THIRD = WQKV // 3


def spread_kernel(dq, out, gkv, tok_in, weight_in, attn, grad_tokens, grad_weight,
                  weight, tok, dq_in, out_in, gkv_own, pair_in, pair_sum, kv_in, tok_perm, gq, product,
                  first_own, first_out, first_in, second_out, second_in, third_out, third_in,
                  fetched, pair_sems, dq_send, dq_recv, out_send, out_recv, kv_send, kv_recv, gq_sems,
                  first_send, first_recv, second_send, second_recv, third_send, third_recv, local):
    dp = lax.axis_index("dp")
    me = lax.axis_index("ctx")
    core = lax.rem(me, 2)
    chip = me // 2
    sibling = (dp, me + 1 - 2 * core)
    place = {"x": dp // 2, "y": (me // 8) * 2 + lax.rem(dp, 2), "z": lax.rem(chip, 4)}

    def neighbour(axis, offset):
        at = lax.rem(place[axis] + offset, 4)
        if axis == "x":
            return (at * 2 + lax.rem(dp, 2), me)
        if axis == "y":
            return ((dp // 2) * 2 + lax.rem(at, 2), (at // 2) * 8 + lax.rem(me, 8))
        return (dp, (me // 8) * 8 + at * 2 + core)

    barrier = pltpu.get_barrier_semaphore()
    greet = [(dp, lax.rem(me + step, HEADS)) for step in range(1, HEADS)]
    greet += [neighbour("x", step) for step in (1, 2, 3)] + [neighbour("y", step) for step in (1, 3)]
    for device in greet:
        pl.semaphore_signal(barrier, inc=1, device_id=device, device_id_type=MESH)
    fetches = [
        pltpu.make_async_copy(gkv.at[:, core], gkv_own, fetched.at[0]),
        pltpu.make_async_copy(tok_in, tok, fetched.at[1]),
        pltpu.make_async_copy(weight_in, weight, fetched.at[2]),
    ]
    for fetch in fetches:
        fetch.start()
    pl.semaphore_wait(barrier, len(greet))

    def remote(src, dst, send, recv, device):
        return pltpu.make_async_remote_copy(
            src_ref=src, dst_ref=dst, send_sem=send, recv_sem=recv, device_id=device, device_id_type=MESH)

    pair_copy = remote(gkv.at[:, 1 - core], pair_in, pair_sems.at[0], pair_sems.at[1], sibling)
    pair_copy.start()
    dq_local = pltpu.make_async_copy(dq.at[me], dq_in.at[me], local.at[0])
    dq_local.start()
    out_local = pltpu.make_async_copy(out.at[me], out_in.at[me], local.at[1])
    out_local.start()

    def dq_copy(peer, slot):
        return remote(dq.at[peer], dq_in.at[slot], dq_send.at[peer], dq_recv.at[slot], (dp, peer))

    def out_copy(peer, slot):
        return remote(out.at[peer], out_in.at[slot], out_send.at[peer], out_recv.at[slot], (dp, peer))

    def kv_copy(to, slot):
        return remote(pair_sum.at[to], kv_in.at[slot], kv_send.at[to], kv_recv.at[slot], (dp, to * 2 + core))

    for step in range(1, HEADS):
        dq_copy(lax.rem(me + step, HEADS), me).start()
    fetches[0].wait()
    pair_copy.wait()
    for step in range(1, 9):
        to = lax.rem(chip + step, 8)
        total = gkv_own[to] + pair_in[to]
        if step < 8:
            pair_sum[to] = total
            kv_copy(to, chip).start()
        else:
            kv_in[chip] = total

    fetches[1].wait()
    for part, order in enumerate(AXES):
        for a in range(4):
            for b in range(4):
                for c in range(4):
                    at = dict(zip(order, (a, b, c)))
                    group = at["x"] * 16 + (at["y"] % 2) * 8 + (at["y"] // 2) * 4 + at["z"]
                    for half in range(2):
                        tok_perm[part, a, (b * 4 + c) * 16:(b * 4 + c + 1) * 16, half * ROWS:(half + 1) * ROWS] = (
                            tok[half, group * 16:(group + 1) * 16, :])

    for step in range(1, HEADS):
        src = lax.rem(me + HEADS - step, HEADS)
        dq_copy(src, src).wait_recv()
    dq_local.wait()

    def two_heads(ref, i):
        first, second = ref[2 * i], ref[2 * i + 1]
        return [jnp.concatenate([first[:, cut], second[:, cut]], axis=1) for cut in (slice(0, 64), slice(64, 128))]

    mine = gq.at[core]
    for i in range(HEADS // 2):
        for half, block in enumerate(two_heads(dq_in, i)):
            mine[half * BLK:(half + 1) * BLK, i * 128:(i + 1) * 128] = block
    for step in range(1, 8):
        src = lax.rem(chip + 8 - step, 8)
        kv_copy(src, src).wait_recv()
    for i in range(KV_HEADS // 2):
        sums = [(kv_in[4 * i + 2 * j] + kv_in[4 * i + 2 * j + 1]).astype(BF16) for j in range(2)]
        mine[:, 1024 + i * 128:1024 + (i + 1) * 128] = jnp.concatenate([s[:, :64] for s in sums], axis=1)
        mine[:, 1280 + i * 128:1280 + (i + 1) * 128] = jnp.concatenate([s[:, 64:] for s in sums], axis=1)
    gq_copy = remote(mine, mine, gq_sems.at[0], gq_sems.at[1], sibling)
    gq_copy.start()
    fetches[2].wait()
    for part in range(8):
        product[:, part * 256:(part + 1) * 256] = lax.dot_general(
            mine[...], weight[part * 256:(part + 1) * 256, :], NT, preferred_element_type=F32).astype(BF16)
    product_copy = pltpu.make_async_copy(product, grad_tokens, local.at[2])
    product_copy.start()
    remote(gq.at[1 - core], gq.at[1 - core], gq_sems.at[0], gq_sems.at[1], sibling).wait_recv()

    def first(part, offset):
        return remote(first_out.at[part, offset - 1], first_in.at[part, offset - 1], first_send.at[part, offset - 1],
                      first_recv.at[part, offset - 1], neighbour(AXES[part][0], offset))

    def later(level, part, offset):
        out_, in_, send, recv = ((second_out, second_in, second_send, second_recv),
                                 (third_out, third_in, third_send, third_recv))[level - 1]
        axis = AXES[part][level]
        return remote(out_.at[part, lax.rem(place[axis] + offset, 4)], in_.at[part, offset - 1],
                      send.at[part, offset - 1], recv.at[part, offset - 1], neighbour(axis, offset))

    for offset in (2, 1, 3, 0):
        for part in range(3):
            to = lax.rem(place[AXES[part][0]] + offset, 4)
            cols = slice(part * THIRD, (part + 1) * THIRD)
            rows = tok_perm.at[part, to]
            term = (jnp.dot(rows[:, :ROWS], gq[0, :, cols], preferred_element_type=F32)
                    + jnp.dot(rows[:, ROWS:], gq[1, :, cols], preferred_element_type=F32))
            if offset:
                first_out[part, offset - 1] = term.astype(BF16)
                first(part, offset).start()
            else:
                first_own[part] = term
    for step in range(1, HEADS):
        out_copy(lax.rem(me + step, HEADS), me).start()

    for part in range(3):
        for offset in (1, 2, 3):
            first(part, offset).wait_recv()
        for b in range(4):
            rows = slice(b * 64, (b + 1) * 64)
            second_out[part, b] = first_own[part, rows] + (
                first_in[part, 0, rows].astype(F32) + first_in[part, 1, rows].astype(F32)
                + first_in[part, 2, rows].astype(F32))
        for offset in (2, 1, 3):
            later(1, part, offset).start()
    for part in range(3):
        own = place[AXES[part][1]]
        for offset in (1, 2, 3):
            later(1, part, offset).wait_recv()
        for c in range(4):
            rows = slice(c * 16, (c + 1) * 16)
            third_out[part, c] = (second_out[part, own, rows] + second_in[part, 0, rows]
                                  + second_in[part, 1, rows] + second_in[part, 2, rows])
        for offset in (2, 1, 3):
            later(2, part, offset).start()

    for step in range(1, HEADS):
        src = lax.rem(me + HEADS - step, HEADS)
        out_copy(src, src).wait_recv()
    out_local.wait()
    for i in range(HEADS // 2):
        for half, block in enumerate(two_heads(out_in, i)):
            attn[half * BLK:(half + 1) * BLK, i * 128:(i + 1) * 128] = block

    for part in range(3):
        own = place[AXES[part][2]]
        for offset in (1, 2, 3):
            later(2, part, offset).wait_recv()
        grad_weight[:, part * THIRD:(part + 1) * THIRD] = (
            third_out[part, own] + third_in[part, 0] + third_in[part, 1] + third_in[part, 2])

    gq_copy.wait_send()
    product_copy.wait()
    for step in range(1, HEADS):
        peer = lax.rem(me + step, HEADS)
        dq_copy(peer, me).wait_send()
        out_copy(peer, me).wait_send()
    for step in range(1, 8):
        kv_copy(lax.rem(chip + step, 8), chip).wait_send()
    for part in range(3):
        for offset in (1, 2, 3):
            first(part, offset).wait_send()
            later(1, part, offset).wait_send()
            later(2, part, offset).wait_send()


def spread(dq, out, gkv, tok, weight):
    vmem = pl.BlockSpec(memory_space=pltpu.VMEM)
    hbm = pl.BlockSpec(memory_space=pltpu.HBM)
    sem = pltpu.SemaphoreType.DMA
    return pl.pallas_call(
        spread_kernel,
        out_shape=[
            jax.ShapeDtypeStruct((ROWS, 1024), BF16),
            jax.ShapeDtypeStruct((ROWS, D), BF16),
            jax.ShapeDtypeStruct((16, WQKV), F32),
        ],
        in_specs=[hbm] * 5,
        out_specs=[vmem, hbm, vmem],
        scratch_shapes=[
            pltpu.VMEM((D, WQKV), BF16),
            pltpu.VMEM((2, D // 2, ROWS), BF16),
            pltpu.VMEM((HEADS, BLK, 128), BF16),
            pltpu.VMEM((HEADS, BLK, 128), BF16),
            pltpu.VMEM((8, ROWS, 128), F32),
            pltpu.VMEM((8, ROWS, 128), F32),
            pltpu.VMEM((8, ROWS, 128), F32),
            pltpu.VMEM((8, ROWS, 128), F32),
            pltpu.VMEM((3, 4, 256, 2 * ROWS), BF16),
            pltpu.VMEM((2, ROWS, WQKV), BF16),
            pltpu.VMEM((ROWS, D), BF16),
            pltpu.VMEM((3, 256, THIRD), F32),
            pltpu.VMEM((3, 3, 256, THIRD), BF16),
            pltpu.VMEM((3, 3, 256, THIRD), BF16),
            pltpu.VMEM((3, 4, 64, THIRD), F32),
            pltpu.VMEM((3, 3, 64, THIRD), F32),
            pltpu.VMEM((3, 4, 16, THIRD), F32),
            pltpu.VMEM((3, 3, 16, THIRD), F32),
            sem((3,)), sem((2,)), sem((HEADS,)), sem((HEADS,)), sem((HEADS,)), sem((HEADS,)), sem((8,)), sem((8,)),
            sem((2,)), sem((3, 3)), sem((3, 3)), sem((3, 3)), sem((3, 3)), sem((3, 3)), sem((3, 3)), sem((3,)),
        ],
        compiler_params=pltpu.CompilerParams(collective_id=1, has_side_effects=True, vmem_limit_bytes=56 << 20),
        cost_estimate=pl.CostEstimate(flops=4 * ROWS * D * WQKV, bytes_accessed=16 << 20, transcendentals=0),
        name="spread",
    )(dq, out, gkv, tok, weight)


def hand_over_kernel(*refs):
    sems = refs[-1]
    copies = [pltpu.make_async_copy(refs[i], refs[3 + i], sems.at[i]) for i in range(3)]
    for copy in copies:
        copy.start()
    for copy in copies:
        copy.wait()


def hand_over(results):
    vmem = pl.BlockSpec(memory_space=pltpu.VMEM)
    hbm = pl.BlockSpec(memory_space=pltpu.HBM)
    return pl.pallas_call(
        hand_over_kernel,
        out_shape=[jax.ShapeDtypeStruct(r.shape, r.dtype) for r in results],
        in_specs=[vmem] * 3,
        out_specs=[hbm] * 3,
        scratch_shapes=[pltpu.SemaphoreType.DMA((3,))],
        cost_estimate=pl.CostEstimate(flops=0, bytes_accessed=3 << 20, transcendentals=0),
        name="hand_over",
    )(*results)


def shards(tokens, qkv_weight, block_place, seg_ids, output_cotangent):
    q, cot, kv, tok = project(tokens, qkv_weight, output_cotangent)
    out, dq, gkv = attend(block_place, seg_ids, q, cot, kv.reshape(PACK, 128))
    return tuple(hand_over(spread(dq, out, gkv.reshape(8, 2, ROWS, 128), tok, qkv_weight)))


def solution(mesh):
    placed = (P(("dp", "ctx"), None), P(), P("dp", None), P("dp", None), P(("dp", "ctx"), None))
    return jax.shard_map(
        shards,
        mesh=mesh,
        in_specs=placed,
        out_specs=(P(("dp", "ctx"), None), P(("dp", "ctx"), None), P(("dp", "ctx"), None)),
        check_vma=False,
    )
```

```python
import functools
import jax
import jax.numpy as jnp
from jax import lax
from jax.experimental import pallas as pl
from jax.experimental.pallas import tpu as pltpu
from jax.sharding import PartitionSpec as P

HEADS = 16
KV_HEADS = 4
WIDTH = 64
BLK = 128
ROWS = 256
PACK = 4096
D = 2048
WQKV = 1536
MESH = pl.DeviceIdType.MESH
NT = (((1,), (1,)), ((), ()))
F32 = jnp.float32
BF16 = jnp.bfloat16


def project_kernel(tokens_in, weight_in, cot_in, q_out, cot_out, kv_out, tok_out,
                   tokens, weight, cot, q_buf, cot_buf, kv_buf, tok_buf,
                   q_send, q_recv, cot_send, cot_recv, kv_send, kv_recv, tok_send, tok_recv, fetched, local):
    dp = lax.axis_index("dp")
    me = lax.axis_index("ctx")
    core = lax.rem(me, 2)
    sibling = me + 1 - 2 * core

    barrier = pltpu.get_barrier_semaphore()
    for step in range(1, HEADS):
        pl.semaphore_signal(barrier, inc=1, device_id=(dp, lax.rem(me + step, HEADS)), device_id_type=MESH)
    fetches = [
        pltpu.make_async_copy(cot_in, cot, fetched.at[0]),
        pltpu.make_async_copy(tokens_in, tokens, fetched.at[1]),
        pltpu.make_async_copy(weight_in.at[:, 1024:], weight.at[:, 1024:], fetched.at[2]),
        pltpu.make_async_copy(weight_in.at[:, :1024], weight.at[:, :1024], fetched.at[3]),
    ]
    for fetch in fetches:
        fetch.start()

    def remote(src, dst, send, recv, peer):
        return pltpu.make_async_remote_copy(
            src_ref=src, dst_ref=dst, send_sem=send, recv_sem=recv, device_id=(dp, peer), device_id_type=MESH)

    def cot_copy(peer, slot):
        return remote(cot_buf.at[peer], cot_out.at[slot], cot_send.at[peer], cot_recv.at[slot], peer)

    def q_copy(peer, slot):
        return remote(q_buf.at[peer], q_out.at[slot], q_send.at[peer], q_recv.at[slot], peer)

    def kv_copy(peer, slot):
        return remote(kv_buf.at[peer // 4], kv_out.at[slot], kv_send.at[peer], kv_recv.at[slot], peer)

    def kv_forward(slot):
        return remote(kv_out.at[slot], kv_out.at[slot], kv_send.at[slot + 1 - 2 * core], kv_recv.at[slot], sibling)

    def fold_rows(columns):
        return jnp.concatenate([columns[:BLK], columns[BLK:]], axis=1)

    fetches[0].wait()
    for h in range(HEADS):
        cot_buf[h] = fold_rows(cot[:, h * 64:(h + 1) * 64])
    pl.semaphore_wait(barrier, HEADS - 1)
    locals_ = [
        pltpu.make_async_copy(cot_buf.at[me], cot_out.at[me], local.at[0]),
        pltpu.make_async_copy(kv_buf.at[me // 4], kv_out.at[me], local.at[1]),
        pltpu.make_async_copy(q_buf.at[me], q_out.at[me], local.at[2]),
        pltpu.make_async_copy(tok_buf.at[core], tok_out.at[core], local.at[3]),
    ]
    locals_[0].start()
    for step in range(1, HEADS):
        cot_copy(lax.rem(me + step, HEADS), me).start()

    def columns(part):
        return jnp.dot(tokens[...], weight[:, part * 256:(part + 1) * 256], preferred_element_type=F32).astype(BF16)

    fetches[1].wait()
    fetches[2].wait()
    keys, values = columns(4), columns(5)
    for k in range(KV_HEADS):
        kv_buf[k] = jnp.concatenate([keys[:, k * 64:(k + 1) * 64], values[:, k * 64:(k + 1) * 64]], axis=1)
    locals_[1].start()
    for step in range(1, 8):
        kv_copy(lax.rem(me + 2 * step, HEADS), me).start()
    kv_copy(sibling, me).start()
    fetches[3].wait()
    for part in range(4):
        queries = columns(part)
        for i in range(4):
            q_buf[part * 4 + i] = fold_rows(queries[:, i * 64:(i + 1) * 64] * 0.125)
    locals_[2].start()
    for step in range(1, HEADS):
        q_copy(lax.rem(me + step, HEADS), me).start()
    for part in range(8):
        turned = tokens[:, part * 256:(part + 1) * 256].T
        for g in range(8):
            for c in range(2):
                tok_buf[c, part * 128 + g * 16: part * 128 + (g + 1) * 16, :] = turned[(2 * g + c) * 16:(2 * g + c + 1) * 16, :]
    locals_[3].start()
    tok_copy = remote(tok_buf.at[1 - core], tok_out.at[core], tok_send, tok_recv, sibling)
    tok_copy.start()
    for step in range(1, 8):
        src = lax.rem(me + HEADS - 2 * step, HEADS)
        kv_copy(src, src).wait_recv()
        kv_forward(src).start()
    for step in range(1, HEADS):
        src = lax.rem(me + HEADS - step, HEADS)
        cot_copy(src, src).wait_recv()
        q_copy(src, src).wait_recv()
    kv_copy(sibling, sibling).wait_recv()
    for step in range(1, 8):
        src = lax.rem(sibling + HEADS - 2 * step, HEADS)
        kv_copy(src, src).wait_recv()
    remote(tok_buf.at[1 - core], tok_out.at[1 - core], tok_send, tok_recv, sibling).wait_recv()
    tok_copy.wait_send()
    for step in range(1, HEADS):
        peer = lax.rem(me + step, HEADS)
        cot_copy(peer, me).wait_send()
        q_copy(peer, me).wait_send()
    for step in range(1, 8):
        peer = lax.rem(me + 2 * step, HEADS)
        kv_copy(peer, me).wait_send()
        kv_forward(peer).wait_send()
    kv_copy(sibling, me).wait_send()
    for copy in locals_:
        copy.wait()


def project(tokens, weight, cot):
    hbm = pl.BlockSpec(memory_space=pltpu.HBM)
    sem = pltpu.SemaphoreType.DMA
    return pl.pallas_call(
        project_kernel,
        out_shape=[
            jax.ShapeDtypeStruct((HEADS, BLK, 128), BF16),
            jax.ShapeDtypeStruct((HEADS, BLK, 128), BF16),
            jax.ShapeDtypeStruct((HEADS, ROWS, 128), BF16),
            jax.ShapeDtypeStruct((2, D // 2, ROWS), BF16),
        ],
        in_specs=[hbm] * 3,
        out_specs=[hbm] * 4,
        scratch_shapes=[
            pltpu.VMEM((ROWS, D), BF16),
            pltpu.VMEM((D, WQKV), BF16),
            pltpu.VMEM((ROWS, 1024), BF16),
            pltpu.VMEM((HEADS, BLK, 128), BF16),
            pltpu.VMEM((HEADS, BLK, 128), BF16),
            pltpu.VMEM((KV_HEADS, ROWS, 128), BF16),
            pltpu.VMEM((2, D // 2, ROWS), BF16),
            sem((HEADS,)), sem((HEADS,)), sem((HEADS,)), sem((HEADS,)), sem((HEADS,)), sem((HEADS,)),
            sem, sem, sem((4,)), sem((4,)),
        ],
        compiler_params=pltpu.CompilerParams(collective_id=0, has_side_effects=True, vmem_limit_bytes=48 << 20),
        cost_estimate=pl.CostEstimate(flops=2 * ROWS * D * WQKV, bytes_accessed=16 << 20, transcendentals=0),
        name="project",
    )(tokens, weight, cot)


TILE = 256
MOST = 9
SIZES = (4, 2, 1)
NEG = -1e30


def attend_kernel(place, seg, q_in, cot_in, kv_in, out, dq, gkv,
                  q, cot, kv, where_, first, x_buf, cot_t, kv_log, kv_t, grad, score, pair, fetched):
    fetches = [pltpu.make_async_copy(src, dst, fetched.at[i])
               for i, (src, dst) in enumerate(((kv_in, kv), (q_in, q), (cot_in, cot)))]
    for fetch in fetches:
        fetch.start()

    def invert(slot, _):
        where_[place[0, slot]] = slot
        return 0
    lax.fori_loop(0, 32, invert, 0)
    first[0] = 0

    def starts(b, _):
        first[b] = jnp.where(seg[0, b] == seg[0, b - 1], first[b - 1], b)
        return 0
    lax.fori_loop(1, 32, starts, 0)

    lane = lax.broadcasted_iota(jnp.int32, (BLK, 128), 1)
    for fetch in fetches:
        fetch.wait()

    def reorder(tile, _):
        for part in range(2):
            b = 2 * tile + part
            slot = where_[b]
            half = lax.rem(slot, 2)
            dst = pl.ds(pl.multiple_of(b * BLK, BLK), BLK)
            row = tile * 512 + part * BLK
            mine = q[slot // 2]
            mine = jnp.where(half == 0, mine, jnp.concatenate([mine[:, 64:], mine[:, :64]], axis=1))
            x_buf[pl.ds(pl.multiple_of(row, BLK), BLK), :] = jnp.where(lane < 64, mine, jnp.zeros_like(mine))
            mine = cot[slot // 2]
            mine = jnp.where(half == 1, mine, jnp.concatenate([mine[:, 64:], mine[:, :64]], axis=1))
            x_buf[pl.ds(pl.multiple_of(row + 256, BLK), BLK), :] = jnp.where(lane < 64, jnp.zeros_like(mine), mine)
            cot_t[:, dst] = mine.T[64:]
            block = kv[pl.ds(pl.multiple_of(slot * BLK, BLK), BLK), :]
            kv_log[dst, :] = block
            kv_t[:, dst] = block.T
            grad[dst, :] = jnp.zeros((BLK, 128), F32)
        return 0
    lax.fori_loop(0, 16, reorder, 0)

    key_row = lax.broadcasted_iota(jnp.int32, (TILE, TILE), 0)
    lane_row = lax.broadcasted_iota(jnp.int32, (1, TILE), 1)

    def rows_of(c, size=1):
        return pl.ds(pl.multiple_of(c * TILE, TILE), size * TILE)

    def fold(s, op):
        return op(s.reshape(s.shape[0] // 8, 8, TILE), axis=0)

    def sweep(count, body, carry):
        at = 0
        for size in SIZES:
            steps = (count - at) // size
            carry = lax.fori_loop(0, steps, lambda i, carry, at=at, size=size: body(at + i * size, size, carry), carry)
            at = at + steps * size
        return carry

    def one_tile(t, _):
        first0, first1 = first[2 * t], first[2 * t + 1]
        begin = first0 // 2
        count = t - begin + 1
        x = x_buf.at[pl.ds(pl.multiple_of(t * 512, 512), 512), :]
        q_first = jnp.where(lane_row < BLK, first0, first1)

        def scores(i, size, carry):
            peak, total = carry
            c = begin + i
            s = lax.dot_general(kv_log[rows_of(c, size), :], x[:TILE, :], NT, preferred_element_type=F32)
            s = jnp.concatenate([
                s[b * BLK:(b + 1) * BLK] + jnp.where(q_first <= 2 * c + b, 0.0, NEG) for b in range(2 * size)], axis=0)
            score[rows_of(i, size), :] = s
            new = jnp.maximum(peak, jnp.max(fold(s, jnp.max), axis=0, keepdims=True))
            total = total * jnp.exp(peak - new) + fold(jnp.exp(s - new), jnp.sum)
            return new, total

        s = lax.dot_general(kv_log[rows_of(t), :], x[:TILE, :], NT, preferred_element_type=F32)
        s = jnp.where((key_row <= lane_row) & (key_row >= (q_first - 2 * t) * BLK), s, NEG)
        score[rows_of(count - 1), :] = s
        peak = jnp.max(fold(s, jnp.max), axis=0, keepdims=True)
        total = fold(jnp.exp(s - peak), jnp.sum)
        peak, total = sweep(count - 1, scores, (peak, total))
        inv = 1.0 / jnp.sum(total, axis=0, keepdims=True)

        def outs(i, size, acc):
            p = jnp.exp(score[rows_of(i, size), :] - peak) * inv
            score[rows_of(i, size), :] = p
            pb = p.astype(BF16)
            pair[rows_of(i, size), TILE:] = pb
            return acc + jnp.dot(kv_t[64:, rows_of(begin + i, size)], pb, preferred_element_type=F32)
        out_t = sweep(count, outs, jnp.zeros((64, TILE), F32)).astype(BF16)
        dots = jnp.sum(cot_t[:, rows_of(t)].astype(F32) * out_t.astype(F32), axis=0, keepdims=True)

        def grads(i, size, acc):
            rows = rows_of(begin + i, size)
            dp = lax.dot_general(kv_log[rows, :], x[TILE:, :], NT, preferred_element_type=F32)
            g = (score[rows_of(i, size), :] * (dp - dots)).astype(BF16)
            pair[rows_of(i, size), :TILE] = g
            grad[rows, :] += jnp.dot(pair[rows_of(i, size), :], x[...], preferred_element_type=F32)
            return acc + jnp.dot(kv_t[:64, rows], g, preferred_element_type=F32)
        dq_t = (sweep(count, grads, jnp.zeros((64, TILE), F32)) * 0.125).astype(BF16)
        for part in range(2):
            slot = where_[2 * t + part]
            side = (lane < 64) == (lax.rem(slot, 2) == 0)
            for turned, to in ((out_t, out), (dq_t, dq)):
                block = turned[:, part * BLK:(part + 1) * BLK]
                block = jnp.concatenate([block, block], axis=0).T
                to[slot // 2] = jnp.where(side, block, to[slot // 2])
        return 0
    lax.fori_loop(0, PACK // TILE, one_tile, 0)

    def finish(slot, _):
        gkv[pl.ds(pl.multiple_of(slot * BLK, BLK), BLK), :] = grad[pl.ds(pl.multiple_of(place[0, slot] * BLK, BLK), BLK), :]
        return 0
    lax.fori_loop(0, 32, finish, 0)


def attend(place, seg, q, cot, kv):
    vmem = pl.BlockSpec(memory_space=pltpu.VMEM)
    smem = pl.BlockSpec(memory_space=pltpu.SMEM)
    hbm = pl.BlockSpec(memory_space=pltpu.HBM)
    return pl.pallas_call(
        attend_kernel,
        out_shape=[
            jax.ShapeDtypeStruct((HEADS, BLK, 128), BF16),
            jax.ShapeDtypeStruct((HEADS, BLK, 128), BF16),
            jax.ShapeDtypeStruct((PACK, 128), F32),
        ],
        in_specs=[smem, smem, hbm, hbm, hbm],
        out_specs=[vmem] * 3,
        scratch_shapes=[
            pltpu.VMEM((HEADS, BLK, 128), BF16),
            pltpu.VMEM((HEADS, BLK, 128), BF16),
            pltpu.VMEM((PACK, 128), BF16),
            pltpu.SMEM((32,), jnp.int32),
            pltpu.SMEM((32,), jnp.int32),
            pltpu.VMEM((2 * PACK, 128), BF16),
            pltpu.VMEM((64, PACK), BF16),
            pltpu.VMEM((PACK, 128), BF16),
            pltpu.VMEM((128, PACK), BF16),
            pltpu.VMEM((PACK, 128), F32),
            pltpu.VMEM((MOST * TILE, TILE), F32),
            pltpu.VMEM((MOST * TILE, 2 * TILE), BF16),
            pltpu.SemaphoreType.DMA((3,)),
        ],
        compiler_params=pltpu.CompilerParams(vmem_limit_bytes=40 << 20),
        cost_estimate=pl.CostEstimate(flops=10 << 30, bytes_accessed=5 << 20, transcendentals=4 << 20),
        name="attend",
    )(place, seg, q, cot, kv)


ORDERS = (("z", "y", "x"), ("y", "x", "z"), ("x", "z", "y"))
PARTS = ((("x", "z", "y"), 0, 640), (("z", "y", "x"), 640, 256), (("y", "x", "z"), 896, 128), (("y", "x", "z"), 1024, 256), (("z", "y", "x"), 1280, 128), (("x", "z", "y"), 1408, 128))
EARLY = [part for part in range(len(PARTS)) if PARTS[part][1] < 1024]
LATE = [part for part in range(len(PARTS)) if PARTS[part][1] >= 1024]


def spread_kernel(dq, out, gkv, tok_in, weight_in, attn, grad_tokens, grad_weight,
                  weight, tok, dq_in, out_in, gkv_own, pair_in, pair_sum, kv_in, tok_perm, gq, product,
                  fetched, pair_sems, dq_send, dq_recv, out_send, out_recv, kv_send, kv_recv, gq_send, gq_recv,
                  part_send, part_recv, local, *parts):
    first_own, first_out, first_in, second_out, second_in, third_out, third_in = [parts[i::7] for i in range(7)]
    dp = lax.axis_index("dp")
    me = lax.axis_index("ctx")
    core = lax.rem(me, 2)
    chip = me // 2
    sibling = (dp, me + 1 - 2 * core)
    place = {"x": dp // 2, "y": (me // 8) * 2 + lax.rem(dp, 2), "z": lax.rem(chip, 4)}

    def neighbour(axis, offset):
        at = lax.rem(place[axis] + offset, 4)
        if axis == "x":
            return (at * 2 + lax.rem(dp, 2), me)
        if axis == "y":
            return ((dp // 2) * 2 + lax.rem(at, 2), (at // 2) * 8 + lax.rem(me, 8))
        return (dp, (me // 8) * 8 + at * 2 + core)

    barrier = pltpu.get_barrier_semaphore()
    greet = [(dp, lax.rem(me + step, HEADS)) for step in range(1, HEADS)]
    greet += [neighbour("x", step) for step in (1, 2, 3)] + [neighbour("y", step) for step in (1, 3)]
    for device in greet:
        pl.semaphore_signal(barrier, inc=1, device_id=device, device_id_type=MESH)
    fetches = [
        pltpu.make_async_copy(gkv.at[:, core], gkv_own, fetched.at[0]),
        pltpu.make_async_copy(tok_in, tok, fetched.at[1]),
        pltpu.make_async_copy(weight_in, weight, fetched.at[2]),
    ]
    for fetch in fetches:
        fetch.start()
    pl.semaphore_wait(barrier, len(greet))

    def remote(src, dst, send, recv, device):
        return pltpu.make_async_remote_copy(
            src_ref=src, dst_ref=dst, send_sem=send, recv_sem=recv, device_id=device, device_id_type=MESH)

    pair_copy = remote(gkv.at[:, 1 - core], pair_in, pair_sems.at[0], pair_sems.at[1], sibling)
    pair_copy.start()
    dq_local = pltpu.make_async_copy(dq.at[me], dq_in.at[me], local.at[0])
    dq_local.start()
    out_local = pltpu.make_async_copy(out.at[me], out_in.at[me], local.at[1])
    out_local.start()

    def dq_copy(peer, slot):
        return remote(dq.at[peer], dq_in.at[slot], dq_send.at[peer], dq_recv.at[slot], (dp, peer))

    def out_copy(peer, slot):
        return remote(out.at[peer], out_in.at[slot], out_send.at[peer], out_recv.at[slot], (dp, peer))

    def kv_copy(to, slot):
        return remote(pair_sum.at[to], kv_in.at[slot], kv_send.at[to], kv_recv.at[slot], (dp, to * 2 + core))

    for step in range(1, HEADS):
        dq_copy(lax.rem(me + step, HEADS), me).start()
    fetches[0].wait()
    pair_copy.wait()
    for step in range(1, 9):
        to = lax.rem(chip + step, 8)
        total = gkv_own[to] + pair_in[to]
        if step < 8:
            pair_sum[to] = total
            kv_copy(to, chip).start()
        else:
            kv_in[chip] = total

    fetches[1].wait()
    for part, order in enumerate(ORDERS):
        for a in range(4):
            for b in range(4):
                for c in range(4):
                    at = dict(zip(order, (a, b, c)))
                    group = at["x"] * 16 + (at["y"] % 2) * 8 + (at["y"] // 2) * 4 + at["z"]
                    for half in range(2):
                        tok_perm[part, a, (b * 4 + c) * 16:(b * 4 + c + 1) * 16, half * ROWS:(half + 1) * ROWS] = (
                            tok[half, group * 16:(group + 1) * 16, :])

    for step in range(1, HEADS):
        src = lax.rem(me + HEADS - step, HEADS)
        dq_copy(src, src).wait_recv()
    dq_local.wait()

    def two_heads(ref, i):
        first, second = ref[2 * i], ref[2 * i + 1]
        return [jnp.concatenate([first[:, cut], second[:, cut]], axis=1) for cut in (slice(0, 64), slice(64, 128))]

    mine, other = gq.at[core], gq.at[1 - core]

    def gq_copy(ref, cut):
        return remote(ref.at[:, cut * 1024:min(cut * 1024 + 1024, WQKV)], ref.at[:, cut * 1024:min(cut * 1024 + 1024, WQKV)],
                      gq_send.at[cut], gq_recv.at[cut], sibling)

    def first(part, offset):
        return remote(first_out[part].at[offset - 1], first_in[part].at[offset - 1], part_send.at[part, 0, offset - 1],
                      part_recv.at[part, 0, offset - 1], neighbour(PARTS[part][0][0], offset))

    def later(level, part, offset):
        out_, in_ = ((second_out, second_in), (third_out, third_in))[level - 1]
        axis = PARTS[part][0][level]
        return remote(out_[part].at[lax.rem(place[axis] + offset, 4)], in_[part].at[offset - 1],
                      part_send.at[part, level, offset - 1], part_recv.at[part, level, offset - 1], neighbour(axis, offset))

    def start_first(chosen):
        for offset in (2, 1, 3, 0):
            for part in chosen:
                order, begin, width = PARTS[part]
                rows = tok_perm.at[ORDERS.index(order), lax.rem(place[order[0]] + offset, 4)]
                term = (jnp.dot(rows[:, :ROWS], gq[0, :, begin:begin + width], preferred_element_type=F32)
                        + jnp.dot(rows[:, ROWS:], gq[1, :, begin:begin + width], preferred_element_type=F32))
                if offset:
                    first_out[part][offset - 1] = term.astype(BF16)
                    first(part, offset).start()
                else:
                    first_own[part][...] = term

    def start_second(chosen):
        for part in chosen:
            for offset in (1, 2, 3):
                first(part, offset).wait_recv()
            came = first_in[part]
            for b in range(4):
                rows = slice(b * 64, (b + 1) * 64)
                second_out[part][b] = first_own[part][rows] + (
                    came[0, rows].astype(F32) + came[1, rows].astype(F32) + came[2, rows].astype(F32))
            for offset in (2, 1, 3):
                later(1, part, offset).start()

    def start_third(chosen):
        for part in chosen:
            own = place[PARTS[part][0][1]]
            for offset in (1, 2, 3):
                later(1, part, offset).wait_recv()
            came = second_in[part]
            for c in range(4):
                rows = slice(c * 16, (c + 1) * 16)
                third_out[part][c] = second_out[part][own, rows] + came[0, rows] + came[1, rows] + came[2, rows]
            for offset in (2, 1, 3):
                later(2, part, offset).start()

    def finish(chosen):
        for part in chosen:
            order, begin, width = PARTS[part]
            for offset in (1, 2, 3):
                later(2, part, offset).wait_recv()
            came = third_in[part]
            grad_weight[:, begin:begin + width] = third_out[part][place[order[2]]] + came[0] + came[1] + came[2]

    for i in range(HEADS // 2):
        for half, block in enumerate(two_heads(dq_in, i)):
            mine[half * BLK:(half + 1) * BLK, i * 128:(i + 1) * 128] = block
    gq_copy(mine, 0).start()
    gq_copy(other, 0).wait_recv()
    start_first(EARLY)

    for step in range(1, 8):
        src = lax.rem(chip + 8 - step, 8)
        kv_copy(src, src).wait_recv()
    for i in range(KV_HEADS // 2):
        sums = [(kv_in[4 * i + 2 * j] + kv_in[4 * i + 2 * j + 1]).astype(BF16) for j in range(2)]
        mine[:, 1024 + i * 128:1024 + (i + 1) * 128] = jnp.concatenate([s[:, :64] for s in sums], axis=1)
        mine[:, 1280 + i * 128:1280 + (i + 1) * 128] = jnp.concatenate([s[:, 64:] for s in sums], axis=1)
    gq_copy(mine, 1).start()
    for step in range(1, HEADS):
        out_copy(lax.rem(me + step, HEADS), me).start()
    gq_copy(other, 1).wait_recv()
    start_first(LATE)

    start_second(EARLY)
    fetches[2].wait()
    for part in range(8):
        product[:, part * 256:(part + 1) * 256] = lax.dot_general(
            mine[...], weight[part * 256:(part + 1) * 256, :], NT, preferred_element_type=F32).astype(BF16)
    product_copy = pltpu.make_async_copy(product, grad_tokens, local.at[2])
    product_copy.start()
    start_second(LATE)
    start_third(EARLY)
    for step in range(1, HEADS):
        src = lax.rem(me + HEADS - step, HEADS)
        out_copy(src, src).wait_recv()
    out_local.wait()
    for i in range(HEADS // 2):
        for half, block in enumerate(two_heads(out_in, i)):
            attn[half * BLK:(half + 1) * BLK, i * 128:(i + 1) * 128] = block
    start_third(LATE)
    finish(EARLY)
    finish(LATE)

    product_copy.wait()
    for cut in range(2):
        gq_copy(mine, cut).wait_send()
    for step in range(1, HEADS):
        peer = lax.rem(me + step, HEADS)
        dq_copy(peer, me).wait_send()
        out_copy(peer, me).wait_send()
    for step in range(1, 8):
        kv_copy(lax.rem(chip + step, 8), chip).wait_send()
    for part in range(len(PARTS)):
        for offset in (1, 2, 3):
            first(part, offset).wait_send()
            later(1, part, offset).wait_send()
            later(2, part, offset).wait_send()


def spread(dq, out, gkv, tok, weight):
    vmem = pl.BlockSpec(memory_space=pltpu.VMEM)
    hbm = pl.BlockSpec(memory_space=pltpu.HBM)
    sem = pltpu.SemaphoreType.DMA
    return pl.pallas_call(
        spread_kernel,
        out_shape=[
            jax.ShapeDtypeStruct((ROWS, 1024), BF16),
            jax.ShapeDtypeStruct((ROWS, D), BF16),
            jax.ShapeDtypeStruct((16, WQKV), F32),
        ],
        in_specs=[hbm] * 5,
        out_specs=[vmem, hbm, vmem],
        scratch_shapes=[
            pltpu.VMEM((D, WQKV), BF16),
            pltpu.VMEM((2, D // 2, ROWS), BF16),
            pltpu.VMEM((HEADS, BLK, 128), BF16),
            pltpu.VMEM((HEADS, BLK, 128), BF16),
            pltpu.VMEM((8, ROWS, 128), F32),
            pltpu.VMEM((8, ROWS, 128), F32),
            pltpu.VMEM((8, ROWS, 128), F32),
            pltpu.VMEM((8, ROWS, 128), F32),
            pltpu.VMEM((3, 4, 256, 2 * ROWS), BF16),
            pltpu.VMEM((2, ROWS, WQKV), BF16),
            pltpu.VMEM((ROWS, D), BF16),
            sem((3,)), sem((2,)), sem((HEADS,)), sem((HEADS,)), sem((HEADS,)), sem((HEADS,)), sem((8,)), sem((8,)),
            sem((2,)), sem((2,)), sem((len(PARTS), 3, 3)), sem((len(PARTS), 3, 3)), sem((3,)),
        ] + [
            pltpu.VMEM(shape, dtype) for _, _, width in PARTS for shape, dtype in (
                ((256, width), F32), ((3, 256, width), BF16), ((3, 256, width), BF16),
                ((4, 64, width), F32), ((3, 64, width), F32), ((4, 16, width), F32), ((3, 16, width), F32))
        ],
        compiler_params=pltpu.CompilerParams(collective_id=1, has_side_effects=True, vmem_limit_bytes=40 << 20),
        cost_estimate=pl.CostEstimate(flops=4 * ROWS * D * WQKV, bytes_accessed=16 << 20, transcendentals=0),
        name="spread",
    )(dq, out, gkv, tok, weight)


def hand_over_kernel(*refs):
    sems = refs[-1]
    copies = [pltpu.make_async_copy(refs[i], refs[3 + i], sems.at[i]) for i in range(3)]
    for copy in copies:
        copy.start()
    for copy in copies:
        copy.wait()


def hand_over(results):
    vmem = pl.BlockSpec(memory_space=pltpu.VMEM)
    hbm = pl.BlockSpec(memory_space=pltpu.HBM)
    return pl.pallas_call(
        hand_over_kernel,
        out_shape=[jax.ShapeDtypeStruct(r.shape, r.dtype) for r in results],
        in_specs=[vmem] * 3,
        out_specs=[hbm] * 3,
        scratch_shapes=[pltpu.SemaphoreType.DMA((3,))],
        compiler_params=pltpu.CompilerParams(vmem_limit_bytes=4 << 20),
        cost_estimate=pl.CostEstimate(flops=0, bytes_accessed=3 << 20, transcendentals=0),
        name="hand_over",
    )(*results)


def shards(tokens, qkv_weight, block_place, seg_ids, output_cotangent):
    q, cot, kv, tok = project(tokens, qkv_weight, output_cotangent)
    out, dq, gkv = attend(block_place, seg_ids, q, cot, kv.reshape(PACK, 128))
    return tuple(hand_over(spread(dq, out, gkv.reshape(8, 2, ROWS, 128), tok, qkv_weight)))


def solution(mesh):
    placed = (P(("dp", "ctx"), None), P(), P("dp", None), P("dp", None), P(("dp", "ctx"), None))
    return jax.shard_map(
        shards,
        mesh=mesh,
        in_specs=placed,
        out_specs=(P(("dp", "ctx"), None), P(("dp", "ctx"), None), P(("dp", "ctx"), None)),
        check_vma=False,
    )
```

```python
import functools
import jax
import jax.numpy as jnp
from jax import lax
from jax.experimental import pallas as pl
from jax.experimental.pallas import tpu as pltpu
from jax.sharding import PartitionSpec as P

HEADS = 16
KV_HEADS = 4
WIDTH = 64
BLK = 128
ROWS = 256
PACK = 4096
D = 2048
WQKV = 1536
MESH = pl.DeviceIdType.MESH
NT = (((1,), (1,)), ((), ()))
F32 = jnp.float32
BF16 = jnp.bfloat16


def project_kernel(tokens_in, weight_in, cot_in, q_out, cot_out, kv_out, tok_out,
                   tokens, weight, cot, q_buf, cot_buf, kv_buf, tok_buf,
                   q_send, q_recv, cot_send, cot_recv, kv_send, kv_recv, tok_send, tok_recv, fetched, local):
    dp = lax.axis_index("dp")
    me = lax.axis_index("ctx")
    core = lax.rem(me, 2)
    sibling = me + 1 - 2 * core

    barrier = pltpu.get_barrier_semaphore()
    for step in range(1, HEADS):
        pl.semaphore_signal(barrier, inc=1, device_id=(dp, lax.rem(me + step, HEADS)), device_id_type=MESH)
    fetches = [
        pltpu.make_async_copy(cot_in, cot, fetched.at[0]),
        pltpu.make_async_copy(tokens_in, tokens, fetched.at[1]),
        pltpu.make_async_copy(weight_in.at[:, 1024:], weight.at[:, 1024:], fetched.at[2]),
        pltpu.make_async_copy(weight_in.at[:, :1024], weight.at[:, :1024], fetched.at[3]),
    ]
    for fetch in fetches:
        fetch.start()

    def remote(src, dst, send, recv, peer):
        return pltpu.make_async_remote_copy(
            src_ref=src, dst_ref=dst, send_sem=send, recv_sem=recv, device_id=(dp, peer), device_id_type=MESH)

    def cot_copy(peer, slot):
        return remote(cot_buf.at[peer], cot_out.at[slot], cot_send.at[peer], cot_recv.at[slot], peer)

    def q_copy(peer, slot):
        return remote(q_buf.at[peer], q_out.at[slot], q_send.at[peer], q_recv.at[slot], peer)

    def kv_copy(peer, slot):
        return remote(kv_buf.at[peer // 4], kv_out.at[slot], kv_send.at[peer], kv_recv.at[slot], peer)

    def kv_forward(slot):
        return remote(kv_out.at[slot], kv_out.at[slot], kv_send.at[slot + 1 - 2 * core], kv_recv.at[slot], sibling)

    def fold_rows(columns):
        return jnp.concatenate([columns[:BLK], columns[BLK:]], axis=1)

    fetches[0].wait()
    for h in range(HEADS):
        cot_buf[h] = fold_rows(cot[:, h * 64:(h + 1) * 64])
    pl.semaphore_wait(barrier, HEADS - 1)
    locals_ = [
        pltpu.make_async_copy(cot_buf.at[me], cot_out.at[me], local.at[0]),
        pltpu.make_async_copy(kv_buf.at[me // 4], kv_out.at[me], local.at[1]),
        pltpu.make_async_copy(q_buf.at[me], q_out.at[me], local.at[2]),
        pltpu.make_async_copy(tok_buf.at[core], tok_out.at[core], local.at[3]),
    ]
    locals_[0].start()
    for step in range(1, HEADS):
        cot_copy(lax.rem(me + step, HEADS), me).start()

    def columns(part):
        return jnp.dot(tokens[...], weight[:, part * 256:(part + 1) * 256], preferred_element_type=F32).astype(BF16)

    fetches[1].wait()
    fetches[2].wait()
    keys, values = columns(4), columns(5)
    for k in range(KV_HEADS):
        kv_buf[k] = jnp.concatenate([keys[:, k * 64:(k + 1) * 64], values[:, k * 64:(k + 1) * 64]], axis=1)
    locals_[1].start()
    for step in range(1, 8):
        kv_copy(lax.rem(me + 2 * step, HEADS), me).start()
    kv_copy(sibling, me).start()
    fetches[3].wait()
    for part in range(4):
        queries = columns(part)
        for i in range(4):
            q_buf[part * 4 + i] = fold_rows(queries[:, i * 64:(i + 1) * 64] * 0.125)
    locals_[2].start()
    for step in range(1, HEADS):
        q_copy(lax.rem(me + step, HEADS), me).start()
    for part in range(8):
        turned = tokens[:, part * 256:(part + 1) * 256].T
        for g in range(8):
            for c in range(2):
                tok_buf[c, part * 128 + g * 16: part * 128 + (g + 1) * 16, :] = turned[(2 * g + c) * 16:(2 * g + c + 1) * 16, :]
    locals_[3].start()
    tok_copy = remote(tok_buf.at[1 - core], tok_out.at[core], tok_send, tok_recv, sibling)
    tok_copy.start()
    for step in range(1, 8):
        src = lax.rem(me + HEADS - 2 * step, HEADS)
        kv_copy(src, src).wait_recv()
        kv_forward(src).start()
    for step in range(1, HEADS):
        src = lax.rem(me + HEADS - step, HEADS)
        cot_copy(src, src).wait_recv()
        q_copy(src, src).wait_recv()
    kv_copy(sibling, sibling).wait_recv()
    for step in range(1, 8):
        src = lax.rem(sibling + HEADS - 2 * step, HEADS)
        kv_copy(src, src).wait_recv()
    remote(tok_buf.at[1 - core], tok_out.at[1 - core], tok_send, tok_recv, sibling).wait_recv()
    tok_copy.wait_send()
    for step in range(1, HEADS):
        peer = lax.rem(me + step, HEADS)
        cot_copy(peer, me).wait_send()
        q_copy(peer, me).wait_send()
    for step in range(1, 8):
        peer = lax.rem(me + 2 * step, HEADS)
        kv_copy(peer, me).wait_send()
        kv_forward(peer).wait_send()
    kv_copy(sibling, me).wait_send()
    for copy in locals_:
        copy.wait()


def project(tokens, weight, cot):
    hbm = pl.BlockSpec(memory_space=pltpu.HBM)
    sem = pltpu.SemaphoreType.DMA
    return pl.pallas_call(
        project_kernel,
        out_shape=[
            jax.ShapeDtypeStruct((HEADS, BLK, 128), BF16),
            jax.ShapeDtypeStruct((HEADS, BLK, 128), BF16),
            jax.ShapeDtypeStruct((HEADS, ROWS, 128), BF16),
            jax.ShapeDtypeStruct((2, D // 2, ROWS), BF16),
        ],
        in_specs=[hbm] * 3,
        out_specs=[hbm] * 4,
        scratch_shapes=[
            pltpu.VMEM((ROWS, D), BF16),
            pltpu.VMEM((D, WQKV), BF16),
            pltpu.VMEM((ROWS, 1024), BF16),
            pltpu.VMEM((HEADS, BLK, 128), BF16),
            pltpu.VMEM((HEADS, BLK, 128), BF16),
            pltpu.VMEM((KV_HEADS, ROWS, 128), BF16),
            pltpu.VMEM((2, D // 2, ROWS), BF16),
            sem((HEADS,)), sem((HEADS,)), sem((HEADS,)), sem((HEADS,)), sem((HEADS,)), sem((HEADS,)),
            sem, sem, sem((4,)), sem((4,)),
        ],
        compiler_params=pltpu.CompilerParams(collective_id=0, has_side_effects=True, vmem_limit_bytes=48 << 20),
        cost_estimate=pl.CostEstimate(flops=2 * ROWS * D * WQKV, bytes_accessed=16 << 20, transcendentals=0),
        name="project",
    )(tokens, weight, cot)


TILE = 256
MOST = 9
SIZES = (4, 2, 1)
NEG = -1e30


def attend_kernel(place, seg, q_in, cot_in, kv_in, out, dq, gkv,
                  q, cot, kv, where_, first, x_buf, cot_t, kv_log, kv_t, grad, expo, tops, pair, fetched):
    fetches = [pltpu.make_async_copy(src, dst, fetched.at[i])
               for i, (src, dst) in enumerate(((kv_in, kv), (q_in, q), (cot_in, cot)))]
    for fetch in fetches:
        fetch.start()

    def invert(slot, _):
        where_[place[0, slot]] = slot
        return 0
    lax.fori_loop(0, 32, invert, 0)
    first[0] = 0

    def starts(b, _):
        first[b] = jnp.where(seg[0, b] == seg[0, b - 1], first[b - 1], b)
        return 0
    lax.fori_loop(1, 32, starts, 0)

    lane = lax.broadcasted_iota(jnp.int32, (BLK, 128), 1)
    for fetch in fetches:
        fetch.wait()

    def reorder(tile, _):
        for part in range(2):
            b = 2 * tile + part
            slot = where_[b]
            half = lax.rem(slot, 2)
            dst = pl.ds(pl.multiple_of(b * BLK, BLK), BLK)
            row = tile * 512 + part * BLK
            mine = q[slot // 2]
            mine = jnp.where(half == 0, mine, jnp.concatenate([mine[:, 64:], mine[:, :64]], axis=1))
            x_buf[pl.ds(pl.multiple_of(row, BLK), BLK), :] = jnp.where(lane < 64, mine, jnp.zeros_like(mine))
            mine = cot[slot // 2]
            mine = jnp.where(half == 1, mine, jnp.concatenate([mine[:, 64:], mine[:, :64]], axis=1))
            x_buf[pl.ds(pl.multiple_of(row + 256, BLK), BLK), :] = jnp.where(lane < 64, jnp.zeros_like(mine), mine)
            cot_t[:, dst] = mine.T[64:]
            block = kv[pl.ds(pl.multiple_of(slot * BLK, BLK), BLK), :]
            kv_log[dst, :] = block
            kv_t[:, dst] = block.T
            grad[dst, :] = jnp.zeros((BLK, 128), F32)
        return 0
    lax.fori_loop(0, 16, reorder, 0, unroll=2)

    key_row = lax.broadcasted_iota(jnp.int32, (TILE, TILE), 0)
    lane_row = lax.broadcasted_iota(jnp.int32, (1, TILE), 1)

    def rows_of(c, size=1):
        return pl.ds(pl.multiple_of(c * TILE, TILE), size * TILE)

    def fold(s, op):
        return op(s.reshape(s.shape[0] // 8, 8, TILE), axis=0)

    def sweep(count, body, carry):
        at = 0
        for size in SIZES:
            steps = (count - at) // size
            carry = lax.fori_loop(0, steps, lambda i, carry, at=at, size=size: body(at + i * size, size, carry), carry)
            at = at + steps * size
        return carry

    def one_tile(t, _):
        first0, first1 = first[2 * t], first[2 * t + 1]
        begin = first0 // 2
        count = t - begin + 1
        x = x_buf.at[pl.ds(pl.multiple_of(t * 512, 512), 512), :]
        q_first = jnp.where(lane_row < BLK, first0, first1)

        def soften(i, size, s, peak, total):
            new = jnp.maximum(peak, jnp.max(fold(s, jnp.max), axis=0, keepdims=True))
            e = jnp.exp(s - new)
            expo[rows_of(i, size), :] = e
            for j in range(size):
                tops[i + j] = jnp.broadcast_to(new, (8, TILE))
            return new, total * jnp.exp(peak - new) + fold(e, jnp.sum)

        def scores(i, size, carry):
            c = begin + i
            s = lax.dot_general(kv_log[rows_of(c, size), :], x[:TILE, :], NT, preferred_element_type=F32)
            s = jnp.concatenate([
                s[b * BLK:(b + 1) * BLK] + jnp.where(q_first <= 2 * c + b, 0.0, NEG) for b in range(2 * size)], axis=0)
            return soften(i, size, s, *carry)

        s = lax.dot_general(kv_log[rows_of(t), :], x[:TILE, :], NT, preferred_element_type=F32)
        s = jnp.where((key_row <= lane_row) & (key_row >= (q_first - 2 * t) * BLK), s, NEG)
        peak, total = soften(count - 1, 1, s, jnp.full((1, TILE), NEG, F32), jnp.zeros((8, TILE), F32))
        peak, total = sweep(count - 1, scores, (peak, total))
        inv = 1.0 / jnp.sum(total, axis=0, keepdims=True)

        def probs(i, size):
            factor = jnp.exp(tops[i][:1] - peak) * inv
            return expo[rows_of(i, size), :] * factor

        def outs(i, size, acc):
            pb = jnp.concatenate([probs(i + j, 1) for j in range(size)], axis=0).astype(BF16)
            pair[rows_of(i, size), TILE:] = pb
            return acc + jnp.dot(kv_t[64:, rows_of(begin + i, size)], pb, preferred_element_type=F32)
        out_t = sweep(count, outs, jnp.zeros((64, TILE), F32)).astype(BF16)
        dots = jnp.sum(cot_t[:, rows_of(t)].astype(F32) * out_t.astype(F32), axis=0, keepdims=True)

        def grads(i, size, acc):
            rows = rows_of(begin + i, size)
            dp = lax.dot_general(kv_log[rows, :], x[TILE:, :], NT, preferred_element_type=F32)
            p = jnp.concatenate([probs(i + j, 1) for j in range(size)], axis=0)
            g = (p * (dp - dots)).astype(BF16)
            pair[rows_of(i, size), :TILE] = g
            grad[rows, :] += jnp.dot(pair[rows_of(i, size), :], x[...], preferred_element_type=F32)
            return acc + jnp.dot(kv_t[:64, rows], g, preferred_element_type=F32)
        dq_t = (sweep(count, grads, jnp.zeros((64, TILE), F32)) * 0.125).astype(BF16)
        for part in range(2):
            slot = where_[2 * t + part]
            side = (lane < 64) == (lax.rem(slot, 2) == 0)
            for turned, to in ((out_t, out), (dq_t, dq)):
                block = turned[:, part * BLK:(part + 1) * BLK]
                block = jnp.concatenate([block, block], axis=0).T
                to[slot // 2] = jnp.where(side, block, to[slot // 2])
        return 0
    lax.fori_loop(0, PACK // TILE, one_tile, 0)

    def finish(slot, _):
        gkv[pl.ds(pl.multiple_of(slot * BLK, BLK), BLK), :] = grad[pl.ds(pl.multiple_of(place[0, slot] * BLK, BLK), BLK), :]
        return 0
    lax.fori_loop(0, 32, finish, 0)


def attend(place, seg, q, cot, kv):
    vmem = pl.BlockSpec(memory_space=pltpu.VMEM)
    smem = pl.BlockSpec(memory_space=pltpu.SMEM)
    hbm = pl.BlockSpec(memory_space=pltpu.HBM)
    return pl.pallas_call(
        attend_kernel,
        out_shape=[
            jax.ShapeDtypeStruct((HEADS, BLK, 128), BF16),
            jax.ShapeDtypeStruct((HEADS, BLK, 128), BF16),
            jax.ShapeDtypeStruct((PACK, 128), F32),
        ],
        in_specs=[smem, smem, hbm, hbm, hbm],
        out_specs=[vmem] * 3,
        scratch_shapes=[
            pltpu.VMEM((HEADS, BLK, 128), BF16),
            pltpu.VMEM((HEADS, BLK, 128), BF16),
            pltpu.VMEM((PACK, 128), BF16),
            pltpu.SMEM((32,), jnp.int32),
            pltpu.SMEM((32,), jnp.int32),
            pltpu.VMEM((2 * PACK, 128), BF16),
            pltpu.VMEM((64, PACK), BF16),
            pltpu.VMEM((PACK, 128), BF16),
            pltpu.VMEM((128, PACK), BF16),
            pltpu.VMEM((PACK, 128), F32),
            pltpu.VMEM((MOST * TILE, TILE), F32),
            pltpu.VMEM((MOST, 8, TILE), F32),
            pltpu.VMEM((MOST * TILE, 2 * TILE), BF16),
            pltpu.SemaphoreType.DMA((3,)),
        ],
        compiler_params=pltpu.CompilerParams(vmem_limit_bytes=40 << 20),
        cost_estimate=pl.CostEstimate(flops=10 << 30, bytes_accessed=5 << 20, transcendentals=4 << 20),
        name="attend",
    )(place, seg, q, cot, kv)


ORDERS = (("z", "y", "x"), ("y", "x", "z"), ("x", "z", "y"))
PARTS = ((("x", "z", "y"), 0, 512), (("z", "y", "x"), 512, 256), (("y", "x", "z"), 768, 256), (("y", "x", "z"), 1024, 256), (("z", "y", "x"), 1280, 128), (("x", "z", "y"), 1408, 128))
EARLY = [part for part in range(len(PARTS)) if PARTS[part][1] < 1024]
LATE = [part for part in range(len(PARTS)) if PARTS[part][1] >= 1024]


def spread_kernel(dq, out, gkv, tok_in, weight_in, attn, grad_tokens, grad_weight,
                  weight, tok, dq_in, out_in, gkv_own, pair_in, pair_sum, kv_in, tok_perm, gq, product, product_acc,
                  fetched, pair_sems, dq_send, dq_recv, out_send, out_recv, kv_send, kv_recv, gq_send, gq_recv,
                  part_send, part_recv, local, *parts):
    first_own, first_out, first_in, second_out, second_in, third_out, third_in = [parts[i::7] for i in range(7)]
    dp = lax.axis_index("dp")
    me = lax.axis_index("ctx")
    core = lax.rem(me, 2)
    chip = me // 2
    sibling = (dp, me + 1 - 2 * core)
    place = {"x": dp // 2, "y": (me // 8) * 2 + lax.rem(dp, 2), "z": lax.rem(chip, 4)}

    def neighbour(axis, offset):
        at = lax.rem(place[axis] + offset, 4)
        if axis == "x":
            return (at * 2 + lax.rem(dp, 2), me)
        if axis == "y":
            return ((dp // 2) * 2 + lax.rem(at, 2), (at // 2) * 8 + lax.rem(me, 8))
        return (dp, (me // 8) * 8 + at * 2 + core)

    barrier = pltpu.get_barrier_semaphore()
    greet = [(dp, lax.rem(me + step, HEADS)) for step in range(1, HEADS)]
    greet += [neighbour("x", step) for step in (1, 2, 3)] + [neighbour("y", step) for step in (1, 3)]
    for device in greet:
        pl.semaphore_signal(barrier, inc=1, device_id=device, device_id_type=MESH)
    fetches = [
        pltpu.make_async_copy(gkv.at[:, core], gkv_own, fetched.at[0]),
        pltpu.make_async_copy(tok_in, tok, fetched.at[1]),
        pltpu.make_async_copy(weight_in, weight, fetched.at[2]),
    ]
    for fetch in fetches:
        fetch.start()
    pl.semaphore_wait(barrier, len(greet))

    def remote(src, dst, send, recv, device):
        return pltpu.make_async_remote_copy(
            src_ref=src, dst_ref=dst, send_sem=send, recv_sem=recv, device_id=device, device_id_type=MESH)

    def pair_copy(to):
        return remote(gkv.at[to, 1 - core], pair_in.at[to], pair_sems.at[0, to], pair_sems.at[1, to], sibling)

    for step in range(1, 9):
        pair_copy(lax.rem(chip + step, 8)).start()
    dq_local = pltpu.make_async_copy(dq.at[me], dq_in.at[me], local.at[0])
    dq_local.start()
    out_local = pltpu.make_async_copy(out.at[me], out_in.at[me], local.at[1])
    out_local.start()

    def dq_copy(peer, slot):
        return remote(dq.at[peer], dq_in.at[slot], dq_send.at[peer], dq_recv.at[slot], (dp, peer))

    def out_copy(peer, slot):
        return remote(out.at[peer], out_in.at[slot], out_send.at[peer], out_recv.at[slot], (dp, peer))

    def kv_copy(to, slot):
        return remote(pair_sum.at[to], kv_in.at[slot], kv_send.at[to], kv_recv.at[slot], (dp, to * 2 + core))

    for step in range(1, HEADS):
        dq_copy(lax.rem(me + step, HEADS), me).start()
    fetches[0].wait()
    for step in range(1, 9):
        to = lax.rem(chip + step, 8)
        pair_copy(to).wait()
        total = (gkv_own[to] + pair_in[to]).astype(pair_sum.dtype)
        if step < 8:
            pair_sum[to] = total
            kv_copy(to, chip).start()
        else:
            kv_in[chip] = total

    fetches[1].wait()
    for part, order in enumerate(ORDERS):
        for a in range(4):
            for b in range(4):
                for c in range(4):
                    at = dict(zip(order, (a, b, c)))
                    group = at["x"] * 16 + (at["y"] % 2) * 8 + (at["y"] // 2) * 4 + at["z"]
                    for half in range(2):
                        tok_perm[part, a, (b * 4 + c) * 16:(b * 4 + c + 1) * 16, half * ROWS:(half + 1) * ROWS] = (
                            tok[half, group * 16:(group + 1) * 16, :])

    for step in range(1, HEADS):
        src = lax.rem(me + HEADS - step, HEADS)
        dq_copy(src, src).wait_recv()
    dq_local.wait()

    def two_heads(ref, i):
        first, second = ref[2 * i], ref[2 * i + 1]
        return [jnp.concatenate([first[:, cut], second[:, cut]], axis=1) for cut in (slice(0, 64), slice(64, 128))]

    mine, other = gq.at[core], gq.at[1 - core]

    def gq_copy(ref, cut):
        return remote(ref.at[:, cut * 1024:min(cut * 1024 + 1024, WQKV)], ref.at[:, cut * 1024:min(cut * 1024 + 1024, WQKV)],
                      gq_send.at[cut], gq_recv.at[cut], sibling)

    def first(part, offset):
        return remote(first_out[part].at[offset - 1], first_in[part].at[offset - 1], part_send.at[part, 0, offset - 1],
                      part_recv.at[part, 0, offset - 1], neighbour(PARTS[part][0][0], offset))

    def later(level, part, offset):
        out_, in_ = ((second_out, second_in), (third_out, third_in))[level - 1]
        axis = PARTS[part][0][level]
        return remote(out_[part].at[lax.rem(place[axis] + offset, 4)], in_[part].at[offset - 1],
                      part_send.at[part, level, offset - 1], part_recv.at[part, level, offset - 1], neighbour(axis, offset))

    def start_first(chosen):
        for offset in (2, 1, 3, 0):
            for part in chosen:
                order, begin, width = PARTS[part]
                rows = tok_perm.at[ORDERS.index(order), lax.rem(place[order[0]] + offset, 4)]
                term = (jnp.dot(rows[:, :ROWS], gq[0, :, begin:begin + width], preferred_element_type=F32)
                        + jnp.dot(rows[:, ROWS:], gq[1, :, begin:begin + width], preferred_element_type=F32))
                if offset:
                    first_out[part][offset - 1] = term.astype(BF16)
                    first(part, offset).start()
                else:
                    first_own[part][...] = term

    def start_second(chosen):
        for part in chosen:
            for offset in (1, 2, 3):
                first(part, offset).wait_recv()
            came = first_in[part]
            for b in range(4):
                rows = slice(b * 64, (b + 1) * 64)
                second_out[part][b] = first_own[part][rows] + (
                    came[0, rows].astype(F32) + came[1, rows].astype(F32) + came[2, rows].astype(F32))
            for offset in (2, 1, 3):
                later(1, part, offset).start()

    def start_third(chosen):
        for part in chosen:
            own = place[PARTS[part][0][1]]
            for offset in (1, 2, 3):
                later(1, part, offset).wait_recv()
            came = second_in[part]
            for c in range(4):
                rows = slice(c * 16, (c + 1) * 16)
                third_out[part][c] = second_out[part][own, rows] + came[0, rows] + came[1, rows] + came[2, rows]
            for offset in (2, 1, 3):
                later(2, part, offset).start()

    def finish(chosen):
        for part in chosen:
            order, begin, width = PARTS[part]
            for offset in (1, 2, 3):
                later(2, part, offset).wait_recv()
            came = third_in[part]
            grad_weight[:, begin:begin + width] = third_out[part][place[order[2]]] + came[0] + came[1] + came[2]

    for i in range(HEADS // 2):
        for half, block in enumerate(two_heads(dq_in, i)):
            mine[half * BLK:(half + 1) * BLK, i * 128:(i + 1) * 128] = block
    gq_copy(mine, 0).start()
    gq_copy(other, 0).wait_recv()
    start_first(EARLY)
    for step in range(1, HEADS):
        out_copy(lax.rem(me + step, HEADS), me).start()
    fetches[2].wait()
    for part in range(8):
        cols = slice(part * 256, (part + 1) * 256)
        product_acc[:, cols] = lax.dot_general(
            mine[:, :1024], weight[cols, :1024], NT, preferred_element_type=F32)

    for step in range(1, 8):
        src = lax.rem(chip + 8 - step, 8)
        kv_copy(src, src).wait_recv()
    for i in range(KV_HEADS // 2):
        sums = [(kv_in[4 * i + 2 * j].astype(F32) + kv_in[4 * i + 2 * j + 1].astype(F32)).astype(BF16) for j in range(2)]
        mine[:, 1024 + i * 128:1024 + (i + 1) * 128] = jnp.concatenate([s[:, :64] for s in sums], axis=1)
        mine[:, 1280 + i * 128:1280 + (i + 1) * 128] = jnp.concatenate([s[:, 64:] for s in sums], axis=1)
    gq_copy(mine, 1).start()
    gq_copy(other, 1).wait_recv()
    start_first(LATE)
    start_second(EARLY)

    for part in range(8):
        cols = slice(part * 256, (part + 1) * 256)
        product[:, cols] = (product_acc[:, cols] + lax.dot_general(
            mine[:, 1024:], weight[cols, 1024:], NT, preferred_element_type=F32)).astype(BF16)
    product_copy = pltpu.make_async_copy(product, grad_tokens, local.at[2])
    product_copy.start()
    start_third(EARLY)
    start_second(LATE)
    for step in range(1, HEADS):
        src = lax.rem(me + HEADS - step, HEADS)
        out_copy(src, src).wait_recv()
    out_local.wait()
    for i in range(HEADS // 2):
        for half, block in enumerate(two_heads(out_in, i)):
            attn[half * BLK:(half + 1) * BLK, i * 128:(i + 1) * 128] = block
    start_third(LATE)
    finish(EARLY)
    finish(LATE)

    product_copy.wait()
    for cut in range(2):
        gq_copy(mine, cut).wait_send()
    for step in range(1, HEADS):
        peer = lax.rem(me + step, HEADS)
        dq_copy(peer, me).wait_send()
        out_copy(peer, me).wait_send()
    for step in range(1, 8):
        kv_copy(lax.rem(chip + step, 8), chip).wait_send()
    for part in range(len(PARTS)):
        for offset in (1, 2, 3):
            first(part, offset).wait_send()
            later(1, part, offset).wait_send()
            later(2, part, offset).wait_send()


def spread(dq, out, gkv, tok, weight):
    vmem = pl.BlockSpec(memory_space=pltpu.VMEM)
    hbm = pl.BlockSpec(memory_space=pltpu.HBM)
    sem = pltpu.SemaphoreType.DMA
    return pl.pallas_call(
        spread_kernel,
        out_shape=[
            jax.ShapeDtypeStruct((ROWS, 1024), BF16),
            jax.ShapeDtypeStruct((ROWS, D), BF16),
            jax.ShapeDtypeStruct((16, WQKV), F32),
        ],
        in_specs=[hbm] * 5,
        out_specs=[vmem, hbm, vmem],
        scratch_shapes=[
            pltpu.VMEM((D, WQKV), BF16),
            pltpu.VMEM((2, D // 2, ROWS), BF16),
            pltpu.VMEM((HEADS, BLK, 128), BF16),
            pltpu.VMEM((HEADS, BLK, 128), BF16),
            pltpu.VMEM((8, ROWS, 128), F32),
            pltpu.VMEM((8, ROWS, 128), F32),
            pltpu.VMEM((8, ROWS, 128), BF16),
            pltpu.VMEM((8, ROWS, 128), BF16),
            pltpu.VMEM((3, 4, 256, 2 * ROWS), BF16),
            pltpu.VMEM((2, ROWS, WQKV), BF16),
            pltpu.VMEM((ROWS, D), BF16),
            pltpu.VMEM((ROWS, D), F32),
            sem((3,)), sem((2, 8)), sem((HEADS,)), sem((HEADS,)), sem((HEADS,)), sem((HEADS,)), sem((8,)), sem((8,)),
            sem((2,)), sem((2,)), sem((len(PARTS), 3, 3)), sem((len(PARTS), 3, 3)), sem((3,)),
        ] + [
            pltpu.VMEM(shape, dtype) for _, _, width in PARTS for shape, dtype in (
                ((256, width), F32), ((3, 256, width), BF16), ((3, 256, width), BF16),
                ((4, 64, width), F32), ((3, 64, width), F32), ((4, 16, width), F32), ((3, 16, width), F32))
        ],
        compiler_params=pltpu.CompilerParams(collective_id=1, has_side_effects=True, vmem_limit_bytes=40 << 20),
        cost_estimate=pl.CostEstimate(flops=4 * ROWS * D * WQKV, bytes_accessed=16 << 20, transcendentals=0),
        name="spread",
    )(dq, out, gkv, tok, weight)


def hand_over_kernel(*refs):
    sems = refs[-1]
    copies = [pltpu.make_async_copy(refs[i], refs[3 + i], sems.at[i]) for i in range(3)]
    for copy in copies:
        copy.start()
    for copy in copies:
        copy.wait()


def hand_over(results):
    vmem = pl.BlockSpec(memory_space=pltpu.VMEM)
    hbm = pl.BlockSpec(memory_space=pltpu.HBM)
    return pl.pallas_call(
        hand_over_kernel,
        out_shape=[jax.ShapeDtypeStruct(r.shape, r.dtype) for r in results],
        in_specs=[vmem] * 3,
        out_specs=[hbm] * 3,
        scratch_shapes=[pltpu.SemaphoreType.DMA((3,))],
        compiler_params=pltpu.CompilerParams(vmem_limit_bytes=4 << 20),
        cost_estimate=pl.CostEstimate(flops=0, bytes_accessed=3 << 20, transcendentals=0),
        name="hand_over",
    )(*results)


def shards(tokens, qkv_weight, block_place, seg_ids, output_cotangent):
    q, cot, kv, tok = project(tokens, qkv_weight, output_cotangent)
    out, dq, gkv = attend(block_place, seg_ids, q, cot, kv.reshape(PACK, 128))
    return tuple(hand_over(spread(dq, out, gkv.reshape(8, 2, ROWS, 128), tok, qkv_weight)))


def solution(mesh):
    placed = (P(("dp", "ctx"), None), P(), P("dp", None), P("dp", None), P(("dp", "ctx"), None))
    return jax.shard_map(
        shards,
        mesh=mesh,
        in_specs=placed,
        out_specs=(P(("dp", "ctx"), None), P(("dp", "ctx"), None), P(("dp", "ctx"), None)),
        check_vma=False,
    )
```

```python
import functools
import jax
import jax.numpy as jnp
from jax import lax
from jax.experimental import pallas as pl
from jax.experimental.pallas import tpu as pltpu
from jax.sharding import PartitionSpec as P

HEADS = 16
KV_HEADS = 4
WIDTH = 64
BLK = 128
ROWS = 256
PACK = 4096
D = 2048
WQKV = 1536
MESH = pl.DeviceIdType.MESH
NT = (((1,), (1,)), ((), ()))
F32 = jnp.float32
BF16 = jnp.bfloat16


def project_kernel(tokens_in, weight_in, cot_in, q_out, cot_out, kv_out, tok_out,
                   tokens, weight, cot, q_buf, cot_buf, kv_buf, tok_buf,
                   q_send, q_recv, cot_send, cot_recv, kv_send, kv_recv, tok_send, tok_recv, fetched, local):
    dp = lax.axis_index("dp")
    me = lax.axis_index("ctx")
    core = lax.rem(me, 2)
    sibling = me + 1 - 2 * core

    barrier = pltpu.get_barrier_semaphore()
    for step in range(1, HEADS):
        pl.semaphore_signal(barrier, inc=1, device_id=(dp, lax.rem(me + step, HEADS)), device_id_type=MESH)
    fetches = [
        pltpu.make_async_copy(cot_in, cot, fetched.at[0]),
        pltpu.make_async_copy(tokens_in, tokens, fetched.at[1]),
        pltpu.make_async_copy(weight_in.at[:, 1024:], weight.at[:, 1024:], fetched.at[2]),
        pltpu.make_async_copy(weight_in.at[:, :1024], weight.at[:, :1024], fetched.at[3]),
    ]
    for fetch in fetches:
        fetch.start()

    def remote(src, dst, send, recv, peer):
        return pltpu.make_async_remote_copy(
            src_ref=src, dst_ref=dst, send_sem=send, recv_sem=recv, device_id=(dp, peer), device_id_type=MESH)

    def cot_copy(peer, slot):
        return remote(cot_buf.at[peer], cot_out.at[slot], cot_send.at[peer], cot_recv.at[slot], peer)

    def q_copy(peer, slot):
        return remote(q_buf.at[peer], q_out.at[slot], q_send.at[peer], q_recv.at[slot], peer)

    def kv_copy(peer, slot):
        return remote(kv_buf.at[peer // 4], kv_out.at[slot], kv_send.at[peer], kv_recv.at[slot], peer)

    def kv_forward(slot):
        return remote(kv_out.at[slot], kv_out.at[slot], kv_send.at[slot + 1 - 2 * core], kv_recv.at[slot], sibling)

    def fold_rows(columns):
        return jnp.concatenate([columns[:BLK], columns[BLK:]], axis=1)

    fetches[0].wait()
    for h in range(HEADS):
        cot_buf[h] = fold_rows(cot[:, h * 64:(h + 1) * 64])
    pl.semaphore_wait(barrier, HEADS - 1)
    locals_ = [
        pltpu.make_async_copy(cot_buf.at[me], cot_out.at[me], local.at[0]),
        pltpu.make_async_copy(kv_buf.at[me // 4], kv_out.at[me], local.at[1]),
        pltpu.make_async_copy(q_buf.at[me], q_out.at[me], local.at[2]),
        pltpu.make_async_copy(tok_buf.at[core], tok_out.at[core], local.at[3]),
    ]
    locals_[0].start()
    for step in range(1, HEADS):
        cot_copy(lax.rem(me + step, HEADS), me).start()

    def columns(part):
        return jnp.dot(tokens[...], weight[:, part * 256:(part + 1) * 256], preferred_element_type=F32).astype(BF16)

    fetches[1].wait()
    fetches[2].wait()
    keys, values = columns(4), columns(5)
    for k in range(KV_HEADS):
        kv_buf[k] = jnp.concatenate([keys[:, k * 64:(k + 1) * 64], values[:, k * 64:(k + 1) * 64]], axis=1)
    locals_[1].start()
    for step in range(1, 8):
        kv_copy(lax.rem(me + 2 * step, HEADS), me).start()
    kv_copy(sibling, me).start()
    fetches[3].wait()
    for part in range(4):
        queries = columns(part)
        for i in range(4):
            q_buf[part * 4 + i] = fold_rows(queries[:, i * 64:(i + 1) * 64] * 0.125)
    locals_[2].start()
    for step in range(1, HEADS):
        q_copy(lax.rem(me + step, HEADS), me).start()
    for part in range(8):
        turned = tokens[:, part * 256:(part + 1) * 256].T
        for g in range(8):
            for c in range(2):
                tok_buf[c, part * 128 + g * 16: part * 128 + (g + 1) * 16, :] = turned[(2 * g + c) * 16:(2 * g + c + 1) * 16, :]
    locals_[3].start()
    tok_copy = remote(tok_buf.at[1 - core], tok_out.at[core], tok_send, tok_recv, sibling)
    tok_copy.start()
    for step in range(1, 8):
        src = lax.rem(me + HEADS - 2 * step, HEADS)
        kv_copy(src, src).wait_recv()
        kv_forward(src).start()
    for step in range(1, HEADS):
        src = lax.rem(me + HEADS - step, HEADS)
        cot_copy(src, src).wait_recv()
        q_copy(src, src).wait_recv()
    kv_copy(sibling, sibling).wait_recv()
    for step in range(1, 8):
        src = lax.rem(sibling + HEADS - 2 * step, HEADS)
        kv_copy(src, src).wait_recv()
    remote(tok_buf.at[1 - core], tok_out.at[1 - core], tok_send, tok_recv, sibling).wait_recv()
    tok_copy.wait_send()
    for step in range(1, HEADS):
        peer = lax.rem(me + step, HEADS)
        cot_copy(peer, me).wait_send()
        q_copy(peer, me).wait_send()
    for step in range(1, 8):
        peer = lax.rem(me + 2 * step, HEADS)
        kv_copy(peer, me).wait_send()
        kv_forward(peer).wait_send()
    kv_copy(sibling, me).wait_send()
    for copy in locals_:
        copy.wait()


def project(tokens, weight, cot):
    hbm = pl.BlockSpec(memory_space=pltpu.HBM)
    sem = pltpu.SemaphoreType.DMA
    return pl.pallas_call(
        project_kernel,
        out_shape=[
            jax.ShapeDtypeStruct((HEADS, BLK, 128), BF16),
            jax.ShapeDtypeStruct((HEADS, BLK, 128), BF16),
            jax.ShapeDtypeStruct((HEADS, ROWS, 128), BF16),
            jax.ShapeDtypeStruct((2, D // 2, ROWS), BF16),
        ],
        in_specs=[hbm] * 3,
        out_specs=[hbm] * 4,
        scratch_shapes=[
            pltpu.VMEM((ROWS, D), BF16),
            pltpu.VMEM((D, WQKV), BF16),
            pltpu.VMEM((ROWS, 1024), BF16),
            pltpu.VMEM((HEADS, BLK, 128), BF16),
            pltpu.VMEM((HEADS, BLK, 128), BF16),
            pltpu.VMEM((KV_HEADS, ROWS, 128), BF16),
            pltpu.VMEM((2, D // 2, ROWS), BF16),
            sem((HEADS,)), sem((HEADS,)), sem((HEADS,)), sem((HEADS,)), sem((HEADS,)), sem((HEADS,)),
            sem, sem, sem((4,)), sem((4,)),
        ],
        compiler_params=pltpu.CompilerParams(collective_id=0, has_side_effects=True, vmem_limit_bytes=48 << 20),
        cost_estimate=pl.CostEstimate(flops=2 * ROWS * D * WQKV, bytes_accessed=16 << 20, transcendentals=0),
        name="project",
    )(tokens, weight, cot)


TILE = 256
MOST = 9
SIZES = (3, 2, 1)
NEG = -1e30


def attend_kernel(place, seg, q_in, cot_in, kv_in, out, dq, gkv,
                  q, cot, kv, where_, first, x_buf, cot_t, kv_log, kv_t, grad, expo, tops, pair, fetched):
    fetches = [pltpu.make_async_copy(src, dst, fetched.at[i])
               for i, (src, dst) in enumerate(((kv_in, kv), (q_in, q), (cot_in, cot)))]
    for fetch in fetches:
        fetch.start()

    def invert(slot, _):
        where_[place[0, slot]] = slot
        return 0
    lax.fori_loop(0, 32, invert, 0)
    first[0] = 0

    def starts(b, _):
        first[b] = jnp.where(seg[0, b] == seg[0, b - 1], first[b - 1], b)
        return 0
    lax.fori_loop(1, 32, starts, 0)

    lane = lax.broadcasted_iota(jnp.int32, (BLK, 128), 1)
    for fetch in fetches:
        fetch.wait()

    def reorder(tile, _):
        for part in range(2):
            b = 2 * tile + part
            slot = where_[b]
            half = lax.rem(slot, 2)
            dst = pl.ds(pl.multiple_of(b * BLK, BLK), BLK)
            row = tile * 512 + part * BLK
            mine = q[slot // 2]
            mine = jnp.where(half == 0, mine, jnp.concatenate([mine[:, 64:], mine[:, :64]], axis=1))
            x_buf[pl.ds(pl.multiple_of(row, BLK), BLK), :] = jnp.where(lane < 64, mine, jnp.zeros_like(mine))
            mine = cot[slot // 2]
            mine = jnp.where(half == 1, mine, jnp.concatenate([mine[:, 64:], mine[:, :64]], axis=1))
            x_buf[pl.ds(pl.multiple_of(row + 256, BLK), BLK), :] = jnp.where(lane < 64, jnp.zeros_like(mine), mine)
            cot_t[:, dst] = mine.T[64:]
            block = kv[pl.ds(pl.multiple_of(slot * BLK, BLK), BLK), :]
            kv_log[dst, :] = block
            kv_t[:, dst] = block.T
            grad[dst, :] = jnp.zeros((BLK, 128), F32)
        return 0
    lax.fori_loop(0, 16, reorder, 0, unroll=2)

    key_row = lax.broadcasted_iota(jnp.int32, (TILE, TILE), 0)
    lane_row = lax.broadcasted_iota(jnp.int32, (1, TILE), 1)

    def rows_of(c, size=1):
        return pl.ds(pl.multiple_of(c * TILE, TILE), size * TILE)

    def fold(s, op):
        return op(s.reshape(s.shape[0] // 8, 8, TILE), axis=0)

    def sweep(count, body, carry):
        at = 0
        for size in SIZES:
            steps = (count - at) // size
            carry = lax.fori_loop(0, steps, lambda i, carry, at=at, size=size: body(at + i * size, size, carry), carry)
            at = at + steps * size
        return carry

    def one_tile(t, _):
        first0, first1 = first[2 * t], first[2 * t + 1]
        begin = first0 // 2
        count = t - begin + 1
        x = x_buf.at[pl.ds(pl.multiple_of(t * 512, 512), 512), :]
        q_first = jnp.where(lane_row < BLK, first0, first1)

        def soften(i, size, s, peak, total):
            new = jnp.maximum(peak, jnp.max(fold(s, jnp.max), axis=0, keepdims=True))
            e = jnp.exp(s - new)
            expo[rows_of(i, size), :] = e
            for j in range(size):
                tops[i + j] = jnp.broadcast_to(new, (8, TILE))
            return new, total * jnp.exp(peak - new) + fold(e, jnp.sum)

        def scores(i, size, carry):
            c = begin + i
            s = lax.dot_general(kv_log[rows_of(c, size), :], x[:TILE, :], NT, preferred_element_type=F32)
            for j in range(size):
                bias = [jnp.where(q_first <= 2 * (c + j) + b, 0.0, NEG) for b in range(2)]
                block = s[j * TILE:(j + 1) * TILE]
                block = jnp.concatenate([block[:BLK] + bias[0], block[BLK:] + bias[1]], axis=0)
                carry = soften(i + j, 1, block, *carry)
            return carry

        s = lax.dot_general(kv_log[rows_of(t), :], x[:TILE, :], NT, preferred_element_type=F32)
        s = jnp.where((key_row <= lane_row) & (key_row >= (q_first - 2 * t) * BLK), s, NEG)
        peak, total = soften(count - 1, 1, s, jnp.full((1, TILE), NEG, F32), jnp.zeros((8, TILE), F32))
        peak, total = sweep(count - 1, scores, (peak, total))
        inv = 1.0 / jnp.sum(total, axis=0, keepdims=True)

        def probs(i, size):
            factor = jnp.exp(tops[i][:1] - peak) * inv
            return expo[rows_of(i, size), :] * factor

        def outs(i, size, acc):
            pb = jnp.concatenate([probs(i + j, 1) for j in range(size)], axis=0).astype(BF16)
            pair[rows_of(i, size), :] = pb
            return acc + jnp.dot(kv_t[64:, rows_of(begin + i, size)], pb, preferred_element_type=F32)
        out_t = sweep(count, outs, jnp.zeros((64, TILE), F32)).astype(BF16)
        dots = jnp.sum(cot_t[:, rows_of(t)].astype(F32) * out_t.astype(F32), axis=0, keepdims=True)

        def grads(i, size, acc):
            rows = rows_of(begin + i, size)
            dp = lax.dot_general(kv_log[rows, :], x[TILE:, :], NT, preferred_element_type=F32)
            p = jnp.concatenate([probs(i + j, 1) for j in range(size)], axis=0)
            g = (p * (dp - dots)).astype(BF16)
            grad[rows, :] += (jnp.dot(g, x[:TILE, :], preferred_element_type=F32)
                              + jnp.dot(pair[rows_of(i, size), :], x[TILE:, :], preferred_element_type=F32))
            return acc + jnp.dot(kv_t[:64, rows], g, preferred_element_type=F32)
        dq_t = (sweep(count, grads, jnp.zeros((64, TILE), F32)) * 0.125).astype(BF16)
        for part in range(2):
            slot = where_[2 * t + part]
            side = (lane < 64) == (lax.rem(slot, 2) == 0)
            for turned, to in ((out_t, out), (dq_t, dq)):
                block = turned[:, part * BLK:(part + 1) * BLK]
                block = jnp.concatenate([block, block], axis=0).T
                to[slot // 2] = jnp.where(side, block, to[slot // 2])
        return 0
    lax.fori_loop(0, PACK // TILE, one_tile, 0)

    def finish(slot, _):
        gkv[pl.ds(pl.multiple_of(slot * BLK, BLK), BLK), :] = grad[pl.ds(pl.multiple_of(place[0, slot] * BLK, BLK), BLK), :]
        return 0
    lax.fori_loop(0, 32, finish, 0)


def attend(place, seg, q, cot, kv):
    vmem = pl.BlockSpec(memory_space=pltpu.VMEM)
    smem = pl.BlockSpec(memory_space=pltpu.SMEM)
    hbm = pl.BlockSpec(memory_space=pltpu.HBM)
    return pl.pallas_call(
        attend_kernel,
        out_shape=[
            jax.ShapeDtypeStruct((HEADS, BLK, 128), BF16),
            jax.ShapeDtypeStruct((HEADS, BLK, 128), BF16),
            jax.ShapeDtypeStruct((PACK, 128), F32),
        ],
        in_specs=[smem, smem, hbm, hbm, hbm],
        out_specs=[vmem] * 3,
        scratch_shapes=[
            pltpu.VMEM((HEADS, BLK, 128), BF16),
            pltpu.VMEM((HEADS, BLK, 128), BF16),
            pltpu.VMEM((PACK, 128), BF16),
            pltpu.SMEM((32,), jnp.int32),
            pltpu.SMEM((32,), jnp.int32),
            pltpu.VMEM((2 * PACK, 128), BF16),
            pltpu.VMEM((64, PACK), BF16),
            pltpu.VMEM((PACK, 128), BF16),
            pltpu.VMEM((128, PACK), BF16),
            pltpu.VMEM((PACK, 128), F32),
            pltpu.VMEM((MOST * TILE, TILE), F32),
            pltpu.VMEM((MOST, 8, TILE), F32),
            pltpu.VMEM((MOST * TILE, TILE), BF16),
            pltpu.SemaphoreType.DMA((3,)),
        ],
        compiler_params=pltpu.CompilerParams(vmem_limit_bytes=40 << 20),
        cost_estimate=pl.CostEstimate(flops=10 << 30, bytes_accessed=5 << 20, transcendentals=4 << 20),
        name="attend",
    )(place, seg, q, cot, kv)


ORDERS = (("z", "y", "x"), ("y", "x", "z"), ("x", "z", "y"))
PARTS = ((("x", "z", "y"), 0, 512), (("z", "y", "x"), 512, 256), (("y", "x", "z"), 768, 256), (("y", "x", "z"), 1024, 256), (("z", "y", "x"), 1280, 128), (("x", "z", "y"), 1408, 128))
EARLY = [part for part in range(len(PARTS)) if PARTS[part][1] < 1024]
LATE = [part for part in range(len(PARTS)) if PARTS[part][1] >= 1024]


def spread_kernel(dq, out, gkv, tok_in, weight_in, attn, grad_tokens, grad_weight,
                  weight, tok, dq_in, out_in, gkv_own, pair_in, pair_sum, kv_in, tok_perm, gq, product,
                  fetched, pair_sems, dq_send, dq_recv, out_send, out_recv, kv_send, kv_recv, gq_send, gq_recv,
                  part_send, part_recv, local, *parts):
    first_own, first_out, first_in, second_out, second_in, third_out, third_in = [parts[i::7] for i in range(7)]
    dp = lax.axis_index("dp")
    me = lax.axis_index("ctx")
    core = lax.rem(me, 2)
    chip = me // 2
    sibling = (dp, me + 1 - 2 * core)
    place = {"x": dp // 2, "y": (me // 8) * 2 + lax.rem(dp, 2), "z": lax.rem(chip, 4)}

    def neighbour(axis, offset):
        at = lax.rem(place[axis] + offset, 4)
        if axis == "x":
            return (at * 2 + lax.rem(dp, 2), me)
        if axis == "y":
            return ((dp // 2) * 2 + lax.rem(at, 2), (at // 2) * 8 + lax.rem(me, 8))
        return (dp, (me // 8) * 8 + at * 2 + core)

    barrier = pltpu.get_barrier_semaphore()
    greet = [(dp, lax.rem(me + step, HEADS)) for step in range(1, HEADS)]
    greet += [neighbour("x", step) for step in (1, 2, 3)] + [neighbour("y", step) for step in (1, 3)]
    for device in greet:
        pl.semaphore_signal(barrier, inc=1, device_id=device, device_id_type=MESH)
    fetches = [
        pltpu.make_async_copy(gkv.at[:, core], gkv_own, fetched.at[0]),
        pltpu.make_async_copy(tok_in, tok, fetched.at[1]),
        pltpu.make_async_copy(weight_in, weight, fetched.at[2]),
    ]
    for fetch in fetches:
        fetch.start()
    pl.semaphore_wait(barrier, len(greet))

    def remote(src, dst, send, recv, device):
        return pltpu.make_async_remote_copy(
            src_ref=src, dst_ref=dst, send_sem=send, recv_sem=recv, device_id=device, device_id_type=MESH)

    pair_copy = remote(gkv.at[:, 1 - core], pair_in, pair_sems.at[0], pair_sems.at[1], sibling)
    pair_copy.start()
    dq_local = pltpu.make_async_copy(dq.at[me], dq_in.at[me], local.at[0])
    dq_local.start()
    out_local = pltpu.make_async_copy(out.at[me], out_in.at[me], local.at[1])
    out_local.start()

    def dq_copy(peer, slot):
        return remote(dq.at[peer], dq_in.at[slot], dq_send.at[peer], dq_recv.at[slot], (dp, peer))

    def out_copy(peer, slot):
        return remote(out.at[peer], out_in.at[slot], out_send.at[peer], out_recv.at[slot], (dp, peer))

    def kv_copy(to, slot):
        return remote(pair_sum.at[to], kv_in.at[slot], kv_send.at[to], kv_recv.at[slot], (dp, to * 2 + core))

    for step in range(1, HEADS):
        dq_copy(lax.rem(me + step, HEADS), me).start()
    fetches[0].wait()
    pair_copy.wait()
    for step in range(1, 9):
        to = lax.rem(chip + step, 8)
        total = gkv_own[to] + pair_in[to]
        if step < 8:
            pair_sum[to] = total
            kv_copy(to, chip).start()
        else:
            kv_in[chip] = total

    fetches[1].wait()
    for part, order in enumerate(ORDERS):
        for a in range(4):
            for b in range(4):
                for c in range(4):
                    at = dict(zip(order, (a, b, c)))
                    group = at["x"] * 16 + (at["y"] % 2) * 8 + (at["y"] // 2) * 4 + at["z"]
                    for half in range(2):
                        tok_perm[part, a, (b * 4 + c) * 16:(b * 4 + c + 1) * 16, half * ROWS:(half + 1) * ROWS] = (
                            tok[half, group * 16:(group + 1) * 16, :])

    for step in range(1, HEADS):
        src = lax.rem(me + HEADS - step, HEADS)
        dq_copy(src, src).wait_recv()
    dq_local.wait()

    def two_heads(ref, i):
        first, second = ref[2 * i], ref[2 * i + 1]
        return [jnp.concatenate([first[:, cut], second[:, cut]], axis=1) for cut in (slice(0, 64), slice(64, 128))]

    mine, other = gq.at[core], gq.at[1 - core]

    def gq_copy(ref, cut):
        return remote(ref.at[:, cut * 1024:min(cut * 1024 + 1024, WQKV)], ref.at[:, cut * 1024:min(cut * 1024 + 1024, WQKV)],
                      gq_send.at[cut], gq_recv.at[cut], sibling)

    def first(part, offset):
        return remote(first_out[part].at[offset - 1], first_in[part].at[offset - 1], part_send.at[part, 0, offset - 1],
                      part_recv.at[part, 0, offset - 1], neighbour(PARTS[part][0][0], offset))

    def later(level, part, offset):
        out_, in_ = ((second_out, second_in), (third_out, third_in))[level - 1]
        axis = PARTS[part][0][level]
        return remote(out_[part].at[lax.rem(place[axis] + offset, 4)], in_[part].at[offset - 1],
                      part_send.at[part, level, offset - 1], part_recv.at[part, level, offset - 1], neighbour(axis, offset))

    def start_first(chosen):
        for offset in (2, 1, 3, 0):
            for part in chosen:
                order, begin, width = PARTS[part]
                rows = tok_perm.at[ORDERS.index(order), lax.rem(place[order[0]] + offset, 4)]
                term = (jnp.dot(rows[:, :ROWS], gq[0, :, begin:begin + width], preferred_element_type=F32)
                        + jnp.dot(rows[:, ROWS:], gq[1, :, begin:begin + width], preferred_element_type=F32))
                if offset:
                    first_out[part][offset - 1] = term.astype(BF16)
                    first(part, offset).start()
                else:
                    first_own[part][...] = term

    def start_second(chosen):
        for part in chosen:
            for offset in (1, 2, 3):
                first(part, offset).wait_recv()
            came = first_in[part]
            for b in range(4):
                rows = slice(b * 64, (b + 1) * 64)
                second_out[part][b] = first_own[part][rows] + (
                    came[0, rows].astype(F32) + came[1, rows].astype(F32) + came[2, rows].astype(F32))
            for offset in (2, 1, 3):
                later(1, part, offset).start()

    def start_third(chosen):
        for part in chosen:
            own = place[PARTS[part][0][1]]
            for offset in (1, 2, 3):
                later(1, part, offset).wait_recv()
            came = second_in[part]
            for c in range(4):
                rows = slice(c * 16, (c + 1) * 16)
                third_out[part][c] = second_out[part][own, rows] + came[0, rows] + came[1, rows] + came[2, rows]
            for offset in (2, 1, 3):
                later(2, part, offset).start()

    def finish(chosen):
        for part in chosen:
            order, begin, width = PARTS[part]
            for offset in (1, 2, 3):
                later(2, part, offset).wait_recv()
            came = third_in[part]
            grad_weight[:, begin:begin + width] = third_out[part][place[order[2]]] + came[0] + came[1] + came[2]

    for i in range(HEADS // 2):
        for half, block in enumerate(two_heads(dq_in, i)):
            mine[half * BLK:(half + 1) * BLK, i * 128:(i + 1) * 128] = block
    gq_copy(mine, 0).start()
    gq_copy(other, 0).wait_recv()
    start_first(EARLY)

    for step in range(1, 8):
        src = lax.rem(chip + 8 - step, 8)
        kv_copy(src, src).wait_recv()
    for i in range(KV_HEADS // 2):
        sums = [(kv_in[4 * i + 2 * j] + kv_in[4 * i + 2 * j + 1]).astype(BF16) for j in range(2)]
        mine[:, 1024 + i * 128:1024 + (i + 1) * 128] = jnp.concatenate([s[:, :64] for s in sums], axis=1)
        mine[:, 1280 + i * 128:1280 + (i + 1) * 128] = jnp.concatenate([s[:, 64:] for s in sums], axis=1)
    gq_copy(mine, 1).start()
    for step in range(1, HEADS):
        out_copy(lax.rem(me + step, HEADS), me).start()
    gq_copy(other, 1).wait_recv()
    start_first(LATE)

    start_second(EARLY)
    start_second(LATE)
    fetches[2].wait()
    for part in range(8):
        product[:, part * 256:(part + 1) * 256] = lax.dot_general(
            mine[...], weight[part * 256:(part + 1) * 256, :], NT, preferred_element_type=F32).astype(BF16)
    product_copy = pltpu.make_async_copy(product, grad_tokens, local.at[2])
    product_copy.start()
    start_third(EARLY)
    for step in range(1, HEADS):
        src = lax.rem(me + HEADS - step, HEADS)
        out_copy(src, src).wait_recv()
    out_local.wait()
    for i in range(HEADS // 2):
        for half, block in enumerate(two_heads(out_in, i)):
            attn[half * BLK:(half + 1) * BLK, i * 128:(i + 1) * 128] = block
    start_third(LATE)
    finish(EARLY)
    finish(LATE)

    product_copy.wait()
    for cut in range(2):
        gq_copy(mine, cut).wait_send()
    for step in range(1, HEADS):
        peer = lax.rem(me + step, HEADS)
        dq_copy(peer, me).wait_send()
        out_copy(peer, me).wait_send()
    for step in range(1, 8):
        kv_copy(lax.rem(chip + step, 8), chip).wait_send()
    for part in range(len(PARTS)):
        for offset in (1, 2, 3):
            first(part, offset).wait_send()
            later(1, part, offset).wait_send()
            later(2, part, offset).wait_send()


def spread(dq, out, gkv, tok, weight):
    vmem = pl.BlockSpec(memory_space=pltpu.VMEM)
    hbm = pl.BlockSpec(memory_space=pltpu.HBM)
    sem = pltpu.SemaphoreType.DMA
    return pl.pallas_call(
        spread_kernel,
        out_shape=[
            jax.ShapeDtypeStruct((ROWS, 1024), BF16),
            jax.ShapeDtypeStruct((ROWS, D), BF16),
            jax.ShapeDtypeStruct((16, WQKV), F32),
        ],
        in_specs=[hbm] * 5,
        out_specs=[vmem, hbm, vmem],
        scratch_shapes=[
            pltpu.VMEM((D, WQKV), BF16),
            pltpu.VMEM((2, D // 2, ROWS), BF16),
            pltpu.VMEM((HEADS, BLK, 128), BF16),
            pltpu.VMEM((HEADS, BLK, 128), BF16),
            pltpu.VMEM((8, ROWS, 128), F32),
            pltpu.VMEM((8, ROWS, 128), F32),
            pltpu.VMEM((8, ROWS, 128), F32),
            pltpu.VMEM((8, ROWS, 128), F32),
            pltpu.VMEM((3, 4, 256, 2 * ROWS), BF16),
            pltpu.VMEM((2, ROWS, WQKV), BF16),
            pltpu.VMEM((ROWS, D), BF16),
            sem((3,)), sem((2,)), sem((HEADS,)), sem((HEADS,)), sem((HEADS,)), sem((HEADS,)), sem((8,)), sem((8,)),
            sem((2,)), sem((2,)), sem((len(PARTS), 3, 3)), sem((len(PARTS), 3, 3)), sem((3,)),
        ] + [
            pltpu.VMEM(shape, dtype) for _, _, width in PARTS for shape, dtype in (
                ((256, width), F32), ((3, 256, width), BF16), ((3, 256, width), BF16),
                ((4, 64, width), F32), ((3, 64, width), F32), ((4, 16, width), F32), ((3, 16, width), F32))
        ],
        compiler_params=pltpu.CompilerParams(collective_id=1, has_side_effects=True, vmem_limit_bytes=40 << 20),
        cost_estimate=pl.CostEstimate(flops=4 * ROWS * D * WQKV, bytes_accessed=16 << 20, transcendentals=0),
        name="spread",
    )(dq, out, gkv, tok, weight)


def hand_over_kernel(*refs):
    sems = refs[-1]
    copies = [pltpu.make_async_copy(refs[i], refs[3 + i], sems.at[i]) for i in range(3)]
    for copy in copies:
        copy.start()
    for copy in copies:
        copy.wait()


def hand_over(results):
    vmem = pl.BlockSpec(memory_space=pltpu.VMEM)
    hbm = pl.BlockSpec(memory_space=pltpu.HBM)
    return pl.pallas_call(
        hand_over_kernel,
        out_shape=[jax.ShapeDtypeStruct(r.shape, r.dtype) for r in results],
        in_specs=[vmem] * 3,
        out_specs=[hbm] * 3,
        scratch_shapes=[pltpu.SemaphoreType.DMA((3,))],
        compiler_params=pltpu.CompilerParams(vmem_limit_bytes=4 << 20),
        cost_estimate=pl.CostEstimate(flops=0, bytes_accessed=3 << 20, transcendentals=0),
        name="hand_over",
    )(*results)


def shards(tokens, qkv_weight, block_place, seg_ids, output_cotangent):
    q, cot, kv, tok = project(tokens, qkv_weight, output_cotangent)
    out, dq, gkv = attend(block_place, seg_ids, q, cot, kv.reshape(PACK, 128))
    return tuple(hand_over(spread(dq, out, gkv.reshape(8, 2, ROWS, 128), tok, qkv_weight)))


def solution(mesh):
    placed = (P(("dp", "ctx"), None), P(), P("dp", None), P("dp", None), P(("dp", "ctx"), None))
    return jax.shard_map(
        shards,
        mesh=mesh,
        in_specs=placed,
        out_specs=(P(("dp", "ctx"), None), P(("dp", "ctx"), None), P(("dp", "ctx"), None)),
        check_vma=False,
    )
```

```python
import functools
import jax
import jax.numpy as jnp
from jax import lax
from jax.experimental import pallas as pl
from jax.experimental.pallas import tpu as pltpu
from jax.sharding import PartitionSpec as P

HEADS = 16
KV_HEADS = 4
WIDTH = 64
BLK = 128
ROWS = 256
PACK = 4096
D = 2048
WQKV = 1536
MESH = pl.DeviceIdType.MESH
NT = (((1,), (1,)), ((), ()))
F32 = jnp.float32
BF16 = jnp.bfloat16


def project_kernel(tokens_in, weight_in, cot_in, q_out, cot_out, kv_out, tok_out,
                   tokens, weight, cot, q_buf, cot_buf, kv_buf, tok_buf,
                   q_send, q_recv, cot_send, cot_recv, kv_send, kv_recv, tok_send, tok_recv, fetched, local):
    dp = lax.axis_index("dp")
    me = lax.axis_index("ctx")
    core = lax.rem(me, 2)
    sibling = me + 1 - 2 * core

    barrier = pltpu.get_barrier_semaphore()
    for step in range(1, HEADS):
        pl.semaphore_signal(barrier, inc=1, device_id=(dp, lax.rem(me + step, HEADS)), device_id_type=MESH)
    fetches = [
        pltpu.make_async_copy(cot_in, cot, fetched.at[0]),
        pltpu.make_async_copy(tokens_in, tokens, fetched.at[1]),
        pltpu.make_async_copy(weight_in.at[:, 1024:], weight.at[:, 1024:], fetched.at[2]),
        pltpu.make_async_copy(weight_in.at[:, :1024], weight.at[:, :1024], fetched.at[3]),
    ]
    for fetch in fetches:
        fetch.start()

    def remote(src, dst, send, recv, peer):
        return pltpu.make_async_remote_copy(
            src_ref=src, dst_ref=dst, send_sem=send, recv_sem=recv, device_id=(dp, peer), device_id_type=MESH)

    def cot_copy(peer, slot):
        return remote(cot_buf.at[peer], cot_out.at[slot], cot_send.at[peer], cot_recv.at[slot], peer)

    def q_copy(peer, slot):
        return remote(q_buf.at[peer], q_out.at[slot], q_send.at[peer], q_recv.at[slot], peer)

    def kv_copy(peer, slot):
        return remote(kv_buf.at[peer // 4], kv_out.at[slot], kv_send.at[peer], kv_recv.at[slot], peer)

    def kv_forward(slot):
        return remote(kv_out.at[slot], kv_out.at[slot], kv_send.at[slot + 1 - 2 * core], kv_recv.at[slot], sibling)

    def fold_rows(columns):
        return jnp.concatenate([columns[:BLK], columns[BLK:]], axis=1)

    fetches[0].wait()
    for h in range(HEADS):
        cot_buf[h] = fold_rows(cot[:, h * 64:(h + 1) * 64])
    pl.semaphore_wait(barrier, HEADS - 1)
    locals_ = [
        pltpu.make_async_copy(cot_buf.at[me], cot_out.at[me], local.at[0]),
        pltpu.make_async_copy(kv_buf.at[me // 4], kv_out.at[me], local.at[1]),
        pltpu.make_async_copy(q_buf.at[me], q_out.at[me], local.at[2]),
        pltpu.make_async_copy(tok_buf.at[core], tok_out.at[core], local.at[3]),
    ]
    locals_[0].start()
    for step in range(1, HEADS):
        cot_copy(lax.rem(me + step, HEADS), me).start()

    def columns(part):
        return jnp.dot(tokens[...], weight[:, part * 256:(part + 1) * 256], preferred_element_type=F32).astype(BF16)

    fetches[1].wait()
    fetches[2].wait()
    keys, values = columns(4), columns(5)
    for k in range(KV_HEADS):
        kv_buf[k] = jnp.concatenate([keys[:, k * 64:(k + 1) * 64], values[:, k * 64:(k + 1) * 64]], axis=1)
    locals_[1].start()
    for step in range(1, 8):
        kv_copy(lax.rem(me + 2 * step, HEADS), me).start()
    kv_copy(sibling, me).start()
    fetches[3].wait()
    for part in range(4):
        queries = columns(part)
        for i in range(4):
            q_buf[part * 4 + i] = fold_rows(queries[:, i * 64:(i + 1) * 64] * 0.125)
    locals_[2].start()
    for step in range(1, HEADS):
        q_copy(lax.rem(me + step, HEADS), me).start()
    for part in range(8):
        turned = tokens[:, part * 256:(part + 1) * 256].T
        for g in range(8):
            for c in range(2):
                tok_buf[c, part * 128 + g * 16: part * 128 + (g + 1) * 16, :] = turned[(2 * g + c) * 16:(2 * g + c + 1) * 16, :]
    locals_[3].start()
    tok_copy = remote(tok_buf.at[1 - core], tok_out.at[core], tok_send, tok_recv, sibling)
    tok_copy.start()
    for step in range(1, 8):
        src = lax.rem(me + HEADS - 2 * step, HEADS)
        kv_copy(src, src).wait_recv()
        kv_forward(src).start()
    for step in range(1, HEADS):
        src = lax.rem(me + HEADS - step, HEADS)
        cot_copy(src, src).wait_recv()
        q_copy(src, src).wait_recv()
    kv_copy(sibling, sibling).wait_recv()
    for step in range(1, 8):
        src = lax.rem(sibling + HEADS - 2 * step, HEADS)
        kv_copy(src, src).wait_recv()
    remote(tok_buf.at[1 - core], tok_out.at[1 - core], tok_send, tok_recv, sibling).wait_recv()
    tok_copy.wait_send()
    for step in range(1, HEADS):
        peer = lax.rem(me + step, HEADS)
        cot_copy(peer, me).wait_send()
        q_copy(peer, me).wait_send()
    for step in range(1, 8):
        peer = lax.rem(me + 2 * step, HEADS)
        kv_copy(peer, me).wait_send()
        kv_forward(peer).wait_send()
    kv_copy(sibling, me).wait_send()
    for copy in locals_:
        copy.wait()


def project(tokens, weight, cot):
    hbm = pl.BlockSpec(memory_space=pltpu.HBM)
    sem = pltpu.SemaphoreType.DMA
    return pl.pallas_call(
        project_kernel,
        out_shape=[
            jax.ShapeDtypeStruct((HEADS, BLK, 128), BF16),
            jax.ShapeDtypeStruct((HEADS, BLK, 128), BF16),
            jax.ShapeDtypeStruct((HEADS, ROWS, 128), BF16),
            jax.ShapeDtypeStruct((2, D // 2, ROWS), BF16),
        ],
        in_specs=[hbm] * 3,
        out_specs=[hbm] * 4,
        scratch_shapes=[
            pltpu.VMEM((ROWS, D), BF16),
            pltpu.VMEM((D, WQKV), BF16),
            pltpu.VMEM((ROWS, 1024), BF16),
            pltpu.VMEM((HEADS, BLK, 128), BF16),
            pltpu.VMEM((HEADS, BLK, 128), BF16),
            pltpu.VMEM((KV_HEADS, ROWS, 128), BF16),
            pltpu.VMEM((2, D // 2, ROWS), BF16),
            sem((HEADS,)), sem((HEADS,)), sem((HEADS,)), sem((HEADS,)), sem((HEADS,)), sem((HEADS,)),
            sem, sem, sem((4,)), sem((4,)),
        ],
        compiler_params=pltpu.CompilerParams(collective_id=0, has_side_effects=True, vmem_limit_bytes=48 << 20),
        cost_estimate=pl.CostEstimate(flops=2 * ROWS * D * WQKV, bytes_accessed=16 << 20, transcendentals=0),
        name="project",
    )(tokens, weight, cot)


TILE = 256
MOST = 9
SIZES = (3, 2, 1)
NEG = -1e30


def attend_kernel(place, seg, q_in, cot_in, kv_in, out, dq, gkv,
                  q, cot, kv, where_, first, x_buf, cot_t, kv_log, kv_t, grad, expo, tops, pair, fetched):
    fetches = [pltpu.make_async_copy(src, dst, fetched.at[i])
               for i, (src, dst) in enumerate(((kv_in, kv), (q_in, q), (cot_in, cot)))]
    for fetch in fetches:
        fetch.start()

    def invert(slot, _):
        where_[place[0, slot]] = slot
        return 0
    lax.fori_loop(0, 32, invert, 0, unroll=8)
    first[0] = 0

    def starts(b, _):
        first[b] = jnp.where(seg[0, b] == seg[0, b - 1], first[b - 1], b)
        return 0
    lax.fori_loop(1, 32, starts, 0, unroll=True)

    lane = lax.broadcasted_iota(jnp.int32, (BLK, 128), 1)
    for fetch in fetches:
        fetch.wait()

    def reorder(tile, _):
        for part in range(2):
            b = 2 * tile + part
            slot = where_[b]
            half = lax.rem(slot, 2)
            dst = pl.ds(pl.multiple_of(b * BLK, BLK), BLK)
            row = tile * 512 + part * BLK
            mine = q[slot // 2]
            mine = jnp.where(half == 0, mine, jnp.concatenate([mine[:, 64:], mine[:, :64]], axis=1))
            x_buf[pl.ds(pl.multiple_of(row, BLK), BLK), :] = jnp.where(lane < 64, mine, jnp.zeros_like(mine))
            mine = cot[slot // 2]
            mine = jnp.where(half == 1, mine, jnp.concatenate([mine[:, 64:], mine[:, :64]], axis=1))
            x_buf[pl.ds(pl.multiple_of(row + 256, BLK), BLK), :] = jnp.where(lane < 64, jnp.zeros_like(mine), mine)
            cot_t[:, dst] = mine.T[64:]
            block = kv[pl.ds(pl.multiple_of(slot * BLK, BLK), BLK), :]
            kv_log[dst, :] = block
            kv_t[:, dst] = block.T
            grad[dst, :] = jnp.zeros((BLK, 128), F32)
        return 0
    lax.fori_loop(0, 16, reorder, 0, unroll=4)

    key_row = lax.broadcasted_iota(jnp.int32, (TILE, TILE), 0)
    lane_row = lax.broadcasted_iota(jnp.int32, (1, TILE), 1)

    def rows_of(c, size=1):
        return pl.ds(pl.multiple_of(c * TILE, TILE), size * TILE)

    def fold(s, op):
        return op(s.reshape(s.shape[0] // 8, 8, TILE), axis=0)

    def sweep(count, body, carry):
        at = 0
        for size in SIZES:
            steps = (count - at) // size
            carry = lax.fori_loop(0, steps, lambda i, carry, at=at, size=size: body(at + i * size, size, carry), carry)
            at = at + steps * size
        return carry

    def one_tile(t, _):
        first0, first1 = first[2 * t], first[2 * t + 1]
        begin = first0 // 2
        count = t - begin + 1
        x = x_buf.at[pl.ds(pl.multiple_of(t * 512, 512), 512), :]
        q_first = jnp.where(lane_row < BLK, first0, first1)

        def soften(i, size, s, peak, total):
            new = jnp.maximum(peak, jnp.max(fold(s, jnp.max), axis=0, keepdims=True))
            e = jnp.exp(s - new)
            expo[rows_of(i, size), :] = e
            for j in range(size):
                tops[i + j] = jnp.broadcast_to(new, (8, TILE))
            return new, total * jnp.exp(peak - new) + fold(e, jnp.sum)

        def scores(i, size, carry):
            c = begin + i
            s = lax.dot_general(kv_log[rows_of(c, size), :], x[:TILE, :], NT, preferred_element_type=F32)
            for j in range(size):
                bias = [jnp.where(q_first <= 2 * (c + j) + b, 0.0, NEG) for b in range(2)]
                block = s[j * TILE:(j + 1) * TILE]
                block = jnp.concatenate([block[:BLK] + bias[0], block[BLK:] + bias[1]], axis=0)
                carry = soften(i + j, 1, block, *carry)
            return carry

        s = lax.dot_general(kv_log[rows_of(t), :], x[:TILE, :], NT, preferred_element_type=F32)
        s = jnp.where((key_row <= lane_row) & (key_row >= (q_first - 2 * t) * BLK), s, NEG)
        peak, total = soften(count - 1, 1, s, jnp.full((1, TILE), NEG, F32), jnp.zeros((8, TILE), F32))
        peak, total = sweep(count - 1, scores, (peak, total))
        inv = 1.0 / jnp.sum(total, axis=0, keepdims=True)

        def probs(i, size):
            factor = jnp.exp(tops[i][:1] - peak) * inv
            return expo[rows_of(i, size), :] * factor

        def outs(i, size, acc):
            pb = jnp.concatenate([probs(i + j, 1) for j in range(size)], axis=0).astype(BF16)
            pair[rows_of(i, size), :] = pb
            return acc + jnp.dot(kv_t[64:, rows_of(begin + i, size)], pb, preferred_element_type=F32)
        out_t = sweep(count, outs, jnp.zeros((64, TILE), F32)).astype(BF16)
        dots = jnp.sum(cot_t[:, rows_of(t)].astype(F32) * out_t.astype(F32), axis=0, keepdims=True)

        def grads(i, size, acc):
            rows = rows_of(begin + i, size)
            dp = lax.dot_general(kv_log[rows, :], x[TILE:, :], NT, preferred_element_type=F32)
            p = jnp.concatenate([probs(i + j, 1) for j in range(size)], axis=0)
            g = (p * (dp - dots)).astype(BF16)
            grad[rows, :] += (jnp.dot(g, x[:TILE, :], preferred_element_type=F32)
                              + jnp.dot(pair[rows_of(i, size), :], x[TILE:, :], preferred_element_type=F32))
            return acc + jnp.dot(kv_t[:64, rows], g, preferred_element_type=F32)
        dq_t = (sweep(count, grads, jnp.zeros((64, TILE), F32)) * 0.125).astype(BF16)
        for part in range(2):
            slot = where_[2 * t + part]
            side = (lane < 64) == (lax.rem(slot, 2) == 0)
            for turned, to in ((out_t, out), (dq_t, dq)):
                block = turned[:, part * BLK:(part + 1) * BLK]
                block = jnp.concatenate([block, block], axis=0).T
                to[slot // 2] = jnp.where(side, block, to[slot // 2])
        return 0
    lax.fori_loop(0, PACK // TILE, one_tile, 0)

    def finish(slot, _):
        gkv[pl.ds(pl.multiple_of(slot * BLK, BLK), BLK), :] = grad[pl.ds(pl.multiple_of(place[0, slot] * BLK, BLK), BLK), :]
        return 0
    lax.fori_loop(0, 32, finish, 0, unroll=4)


def attend(place, seg, q, cot, kv):
    vmem = pl.BlockSpec(memory_space=pltpu.VMEM)
    smem = pl.BlockSpec(memory_space=pltpu.SMEM)
    hbm = pl.BlockSpec(memory_space=pltpu.HBM)
    return pl.pallas_call(
        attend_kernel,
        out_shape=[
            jax.ShapeDtypeStruct((HEADS, BLK, 128), BF16),
            jax.ShapeDtypeStruct((HEADS, BLK, 128), BF16),
            jax.ShapeDtypeStruct((PACK, 128), F32),
        ],
        in_specs=[smem, smem, hbm, hbm, hbm],
        out_specs=[vmem] * 3,
        scratch_shapes=[
            pltpu.VMEM((HEADS, BLK, 128), BF16),
            pltpu.VMEM((HEADS, BLK, 128), BF16),
            pltpu.VMEM((PACK, 128), BF16),
            pltpu.SMEM((32,), jnp.int32),
            pltpu.SMEM((32,), jnp.int32),
            pltpu.VMEM((2 * PACK, 128), BF16),
            pltpu.VMEM((64, PACK), BF16),
            pltpu.VMEM((PACK, 128), BF16),
            pltpu.VMEM((128, PACK), BF16),
            pltpu.VMEM((PACK, 128), F32),
            pltpu.VMEM((MOST * TILE, TILE), F32),
            pltpu.VMEM((MOST, 8, TILE), F32),
            pltpu.VMEM((MOST * TILE, TILE), BF16),
            pltpu.SemaphoreType.DMA((3,)),
        ],
        compiler_params=pltpu.CompilerParams(vmem_limit_bytes=40 << 20),
        cost_estimate=pl.CostEstimate(flops=10 << 30, bytes_accessed=5 << 20, transcendentals=4 << 20),
        name="attend",
    )(place, seg, q, cot, kv)


ORDERS = (("z", "y", "x"), ("y", "x", "z"), ("x", "z", "y"))
PARTS = ((("x", "z", "y"), 0, 512), (("z", "y", "x"), 512, 256), (("y", "x", "z"), 768, 256), (("y", "x", "z"), 1024, 256), (("z", "y", "x"), 1280, 128), (("x", "z", "y"), 1408, 128))
EARLY = [part for part in range(len(PARTS)) if PARTS[part][1] < 1024]
LATE = [part for part in range(len(PARTS)) if PARTS[part][1] >= 1024]


def spread_kernel(dq, out, gkv, tok_in, weight_in, attn, grad_tokens, grad_weight,
                  weight, tok, dq_in, out_in, gkv_own, pair_in, pair_sum, kv_in, tok_perm, gq, product,
                  fetched, pair_sems, dq_send, dq_recv, out_send, out_recv, kv_send, kv_recv, gq_send, gq_recv,
                  part_send, part_recv, local, *parts):
    first_own, first_out, first_in, second_out, second_in, third_out, third_in = [parts[i::7] for i in range(7)]
    dp = lax.axis_index("dp")
    me = lax.axis_index("ctx")
    core = lax.rem(me, 2)
    chip = me // 2
    sibling = (dp, me + 1 - 2 * core)
    place = {"x": dp // 2, "y": (me // 8) * 2 + lax.rem(dp, 2), "z": lax.rem(chip, 4)}

    def neighbour(axis, offset):
        at = lax.rem(place[axis] + offset, 4)
        if axis == "x":
            return (at * 2 + lax.rem(dp, 2), me)
        if axis == "y":
            return ((dp // 2) * 2 + lax.rem(at, 2), (at // 2) * 8 + lax.rem(me, 8))
        return (dp, (me // 8) * 8 + at * 2 + core)

    barrier = pltpu.get_barrier_semaphore()
    greet = [(dp, lax.rem(me + step, HEADS)) for step in range(1, HEADS)]
    greet += [neighbour("x", step) for step in (1, 2, 3)] + [neighbour("y", step) for step in (1, 3)]
    for device in greet:
        pl.semaphore_signal(barrier, inc=1, device_id=device, device_id_type=MESH)
    fetches = [
        pltpu.make_async_copy(gkv.at[:, core], gkv_own, fetched.at[0]),
        pltpu.make_async_copy(tok_in, tok, fetched.at[1]),
        pltpu.make_async_copy(weight_in, weight, fetched.at[2]),
    ]
    for fetch in fetches:
        fetch.start()
    pl.semaphore_wait(barrier, len(greet))

    def remote(src, dst, send, recv, device):
        return pltpu.make_async_remote_copy(
            src_ref=src, dst_ref=dst, send_sem=send, recv_sem=recv, device_id=device, device_id_type=MESH)

    pair_copy = remote(gkv.at[:, 1 - core], pair_in, pair_sems.at[0], pair_sems.at[1], sibling)
    pair_copy.start()
    dq_local = pltpu.make_async_copy(dq.at[me], dq_in.at[me], local.at[0])
    dq_local.start()
    out_local = pltpu.make_async_copy(out.at[me], out_in.at[me], local.at[1])
    out_local.start()

    def dq_copy(peer, slot):
        return remote(dq.at[peer], dq_in.at[slot], dq_send.at[peer], dq_recv.at[slot], (dp, peer))

    def out_copy(peer, slot):
        return remote(out.at[peer], out_in.at[slot], out_send.at[peer], out_recv.at[slot], (dp, peer))

    def kv_copy(to, slot):
        return remote(pair_sum.at[to], kv_in.at[slot], kv_send.at[to], kv_recv.at[slot], (dp, to * 2 + core))

    for step in range(1, HEADS):
        dq_copy(lax.rem(me + step, HEADS), me).start()
    fetches[0].wait()
    pair_copy.wait()
    for step in range(1, 9):
        to = lax.rem(chip + step, 8)
        total = gkv_own[to] + pair_in[to]
        if step < 8:
            pair_sum[to] = total
            kv_copy(to, chip).start()
        else:
            kv_in[chip] = total

    fetches[1].wait()
    for part, order in enumerate(ORDERS):
        for a in range(4):
            for b in range(4):
                for c in range(4):
                    at = dict(zip(order, (a, b, c)))
                    group = at["x"] * 16 + (at["y"] % 2) * 8 + (at["y"] // 2) * 4 + at["z"]
                    for half in range(2):
                        tok_perm[part, a, (b * 4 + c) * 16:(b * 4 + c + 1) * 16, half * ROWS:(half + 1) * ROWS] = (
                            tok[half, group * 16:(group + 1) * 16, :])

    for step in range(1, HEADS):
        src = lax.rem(me + HEADS - step, HEADS)
        dq_copy(src, src).wait_recv()
    dq_local.wait()

    def two_heads(ref, i):
        first, second = ref[2 * i], ref[2 * i + 1]
        return [jnp.concatenate([first[:, cut], second[:, cut]], axis=1) for cut in (slice(0, 64), slice(64, 128))]

    mine, other = gq.at[core], gq.at[1 - core]

    def gq_copy(ref, cut):
        return remote(ref.at[:, cut * 1024:min(cut * 1024 + 1024, WQKV)], ref.at[:, cut * 1024:min(cut * 1024 + 1024, WQKV)],
                      gq_send.at[cut], gq_recv.at[cut], sibling)

    def first(part, offset):
        return remote(first_out[part].at[offset - 1], first_in[part].at[offset - 1], part_send.at[part, 0, offset - 1],
                      part_recv.at[part, 0, offset - 1], neighbour(PARTS[part][0][0], offset))

    def later(level, part, offset):
        out_, in_ = ((second_out, second_in), (third_out, third_in))[level - 1]
        axis = PARTS[part][0][level]
        return remote(out_[part].at[lax.rem(place[axis] + offset, 4)], in_[part].at[offset - 1],
                      part_send.at[part, level, offset - 1], part_recv.at[part, level, offset - 1], neighbour(axis, offset))

    def start_first(chosen):
        for offset in (2, 1, 3, 0):
            for part in chosen:
                order, begin, width = PARTS[part]
                rows = tok_perm.at[ORDERS.index(order), lax.rem(place[order[0]] + offset, 4)]
                term = (jnp.dot(rows[:, :ROWS], gq[0, :, begin:begin + width], preferred_element_type=F32)
                        + jnp.dot(rows[:, ROWS:], gq[1, :, begin:begin + width], preferred_element_type=F32))
                if offset:
                    first_out[part][offset - 1] = term.astype(BF16)
                    first(part, offset).start()
                else:
                    first_own[part][...] = term

    def start_second(chosen):
        for part in chosen:
            for offset in (1, 2, 3):
                first(part, offset).wait_recv()
            came = first_in[part]
            for b in range(4):
                rows = slice(b * 64, (b + 1) * 64)
                second_out[part][b] = first_own[part][rows] + (
                    came[0, rows].astype(F32) + came[1, rows].astype(F32) + came[2, rows].astype(F32))
            for offset in (2, 1, 3):
                later(1, part, offset).start()

    def start_third(chosen):
        for part in chosen:
            own = place[PARTS[part][0][1]]
            for offset in (1, 2, 3):
                later(1, part, offset).wait_recv()
            came = second_in[part]
            for c in range(4):
                rows = slice(c * 16, (c + 1) * 16)
                third_out[part][c] = second_out[part][own, rows] + came[0, rows] + came[1, rows] + came[2, rows]
            for offset in (2, 1, 3):
                later(2, part, offset).start()

    def finish(chosen):
        for part in chosen:
            order, begin, width = PARTS[part]
            for offset in (1, 2, 3):
                later(2, part, offset).wait_recv()
            came = third_in[part]
            grad_weight[:, begin:begin + width] = third_out[part][place[order[2]]] + came[0] + came[1] + came[2]

    for i in range(HEADS // 2):
        for half, block in enumerate(two_heads(dq_in, i)):
            mine[half * BLK:(half + 1) * BLK, i * 128:(i + 1) * 128] = block
    gq_copy(mine, 0).start()
    gq_copy(other, 0).wait_recv()
    start_first(EARLY)

    for step in range(1, 8):
        src = lax.rem(chip + 8 - step, 8)
        kv_copy(src, src).wait_recv()
    for i in range(KV_HEADS // 2):
        sums = [(kv_in[4 * i + 2 * j] + kv_in[4 * i + 2 * j + 1]).astype(BF16) for j in range(2)]
        mine[:, 1024 + i * 128:1024 + (i + 1) * 128] = jnp.concatenate([s[:, :64] for s in sums], axis=1)
        mine[:, 1280 + i * 128:1280 + (i + 1) * 128] = jnp.concatenate([s[:, 64:] for s in sums], axis=1)
    gq_copy(mine, 1).start()
    for step in range(1, HEADS):
        out_copy(lax.rem(me + step, HEADS), me).start()
    gq_copy(other, 1).wait_recv()
    start_first(LATE)

    start_second(EARLY)
    start_second(LATE)
    fetches[2].wait()
    for part in range(8):
        product[:, part * 256:(part + 1) * 256] = lax.dot_general(
            mine[...], weight[part * 256:(part + 1) * 256, :], NT, preferred_element_type=F32).astype(BF16)
    product_copy = pltpu.make_async_copy(product, grad_tokens, local.at[2])
    product_copy.start()
    start_third(EARLY)
    for step in range(1, HEADS):
        src = lax.rem(me + HEADS - step, HEADS)
        out_copy(src, src).wait_recv()
    out_local.wait()
    for i in range(HEADS // 2):
        for half, block in enumerate(two_heads(out_in, i)):
            attn[half * BLK:(half + 1) * BLK, i * 128:(i + 1) * 128] = block
    start_third(LATE)
    finish(EARLY)
    finish(LATE)

    product_copy.wait()
    for cut in range(2):
        gq_copy(mine, cut).wait_send()
    for step in range(1, HEADS):
        peer = lax.rem(me + step, HEADS)
        dq_copy(peer, me).wait_send()
        out_copy(peer, me).wait_send()
    for step in range(1, 8):
        kv_copy(lax.rem(chip + step, 8), chip).wait_send()
    for part in range(len(PARTS)):
        for offset in (1, 2, 3):
            first(part, offset).wait_send()
            later(1, part, offset).wait_send()
            later(2, part, offset).wait_send()


def spread(dq, out, gkv, tok, weight):
    vmem = pl.BlockSpec(memory_space=pltpu.VMEM)
    hbm = pl.BlockSpec(memory_space=pltpu.HBM)
    sem = pltpu.SemaphoreType.DMA
    return pl.pallas_call(
        spread_kernel,
        out_shape=[
            jax.ShapeDtypeStruct((ROWS, 1024), BF16),
            jax.ShapeDtypeStruct((ROWS, D), BF16),
            jax.ShapeDtypeStruct((16, WQKV), F32),
        ],
        in_specs=[hbm] * 5,
        out_specs=[vmem, hbm, vmem],
        scratch_shapes=[
            pltpu.VMEM((D, WQKV), BF16),
            pltpu.VMEM((2, D // 2, ROWS), BF16),
            pltpu.VMEM((HEADS, BLK, 128), BF16),
            pltpu.VMEM((HEADS, BLK, 128), BF16),
            pltpu.VMEM((8, ROWS, 128), F32),
            pltpu.VMEM((8, ROWS, 128), F32),
            pltpu.VMEM((8, ROWS, 128), F32),
            pltpu.VMEM((8, ROWS, 128), F32),
            pltpu.VMEM((3, 4, 256, 2 * ROWS), BF16),
            pltpu.VMEM((2, ROWS, WQKV), BF16),
            pltpu.VMEM((ROWS, D), BF16),
            sem((3,)), sem((2,)), sem((HEADS,)), sem((HEADS,)), sem((HEADS,)), sem((HEADS,)), sem((8,)), sem((8,)),
            sem((2,)), sem((2,)), sem((len(PARTS), 3, 3)), sem((len(PARTS), 3, 3)), sem((3,)),
        ] + [
            pltpu.VMEM(shape, dtype) for _, _, width in PARTS for shape, dtype in (
                ((256, width), F32), ((3, 256, width), BF16), ((3, 256, width), BF16),
                ((4, 64, width), F32), ((3, 64, width), F32), ((4, 16, width), F32), ((3, 16, width), F32))
        ],
        compiler_params=pltpu.CompilerParams(collective_id=1, has_side_effects=True, vmem_limit_bytes=40 << 20),
        cost_estimate=pl.CostEstimate(flops=4 * ROWS * D * WQKV, bytes_accessed=16 << 20, transcendentals=0),
        name="spread",
    )(dq, out, gkv, tok, weight)


def hand_over_kernel(*refs):
    sems = refs[-1]
    copies = [pltpu.make_async_copy(refs[i], refs[3 + i], sems.at[i]) for i in range(3)]
    for copy in copies:
        copy.start()
    for copy in copies:
        copy.wait()


def hand_over(results):
    vmem = pl.BlockSpec(memory_space=pltpu.VMEM)
    hbm = pl.BlockSpec(memory_space=pltpu.HBM)
    return pl.pallas_call(
        hand_over_kernel,
        out_shape=[jax.ShapeDtypeStruct(r.shape, r.dtype) for r in results],
        in_specs=[vmem] * 3,
        out_specs=[hbm] * 3,
        scratch_shapes=[pltpu.SemaphoreType.DMA((3,))],
        compiler_params=pltpu.CompilerParams(vmem_limit_bytes=4 << 20),
        cost_estimate=pl.CostEstimate(flops=0, bytes_accessed=3 << 20, transcendentals=0),
        name="hand_over",
    )(*results)


def shards(tokens, qkv_weight, block_place, seg_ids, output_cotangent):
    q, cot, kv, tok = project(tokens, qkv_weight, output_cotangent)
    out, dq, gkv = attend(block_place, seg_ids, q, cot, kv.reshape(PACK, 128))
    return tuple(hand_over(spread(dq, out, gkv.reshape(8, 2, ROWS, 128), tok, qkv_weight)))


def solution(mesh):
    placed = (P(("dp", "ctx"), None), P(), P("dp", None), P("dp", None), P(("dp", "ctx"), None))
    return jax.shard_map(
        shards,
        mesh=mesh,
        in_specs=placed,
        out_specs=(P(("dp", "ctx"), None), P(("dp", "ctx"), None), P(("dp", "ctx"), None)),
        check_vma=False,
    )
```
